128 devices in a mesh: tm: 16 (over x, y), ha: 8 (over z, core).
Axes of the slice: x: 4, y: 4, z: 4, core: 2. Of those that a mesh axis runs over, the one named last changes fastest.
Arguments:
- tokens: bfloat16 [32, 8, 16, 16, 1536], P('tm', 'ha'), may hold values from -12 to 12
- projection: bfloat16 [1536, 2304], replicated, may hold values from -0.15309311 to 0.15309311, as said below
- norm_gain: float32 [2, 768], replicated, may hold values from 0.4 to 6.25, as said below
- modulation: float32 [50, 2, 1536], replicated, may hold values from -3 to 3
- levels: int32 [32], P('tm'), may hold values from 0 to 49
- frame_order: int32 [32], replicated, may hold values from 0 to 31, each once
Outputs:
- attended: bfloat16 [32, 8, 16, 16, 768], P('tm', 'ha')
The draws below stay inside these ranges and needn't reach their ends.
Inputs may be any that keep to these rules, and one draw needn't show every extreme that they name: `projection`: each column block has entries of order D ** -0.5. `norm_gain`: positive gains. `frame_order`: each number of 0 to 31 once.
All inputs are finite; a program needn't handle non-finite values.
Results may differ from the reference program's by a relative error of at most 0.0059.
Values may be sent and summed in bfloat16 or wider, within the bound.
No kernel may reach another device: no remote copies, remote signals or barrier semaphores. Data moves between devices by JAX's collectives and lax.ppermute only.
A program may use at most 192 MiB of HBM per device.

```python
import math
import jax
import jax.numpy as jnp
from jax import lax

D = 1536
HEADS = 6
HD = 128
TILE = 16
PAD = 2
TROWS = 2
LEVELS = 50
QD = 768
TILES = 8
FRAMES = 32


def draw_tokens(key, part):
    key = jax.random.fold_in(key, 11)
    key_base = jax.random.fold_in(key, 0)
    shape = (FRAMES, TILES, TILE, TILE, D)
    normal_part = jax.random.normal(key_base, shape, jnp.float32)
    return jnp.clip(normal_part, -12.0, 12.0).astype(jnp.bfloat16)


def draw_projection(key, part):
    key = jax.random.fold_in(key, 23)
    key_query, key_key, key_value = jax.random.split(key, 3)
    query_part = jax.random.normal(key_query, (D, QD), jnp.float32)
    key_part = jax.random.normal(key_key, (D, QD), jnp.float32)
    value_part = jax.random.normal(key_value, (D, QD), jnp.float32)
    joined = jnp.concatenate([query_part, key_part, value_part], axis=1)
    return (jnp.clip(joined, -6.0, 6.0) / math.sqrt(D)).astype(jnp.bfloat16)


def draw_norm_gain(key, part):
    key = jax.random.fold_in(key, 37)
    key_head, key_jitter = jax.random.split(key, 2)
    head_level = jnp.exp(jax.random.uniform(key_head, (HEADS,), jnp.float32, math.log(0.5), math.log(2.5)))
    jitter = jnp.exp(jax.random.uniform(key_jitter, (2, HEADS, HD), jnp.float32, math.log(0.8), math.log(1.25)))
    return (head_level[None, :, None] * jitter).reshape(2, HEADS * HD).astype(jnp.float32)


def set_ends(drawn, stream_key, smallest, largest):
    longest = drawn.shape.index(max(drawn.shape))
    spots = []
    for shift in (0, 1):
        where = [jax.random.randint(jax.random.fold_in(stream_key, axis), (), 0, length) for axis, length in enumerate(drawn.shape)]
        where[longest] = (where[longest] + shift) % drawn.shape[longest]
        spots.append(tuple(where))
    return drawn.at[spots[0]].set(smallest).at[spots[1]].set(largest)


def gaussian(stream_key, shape, deviation, reach, held_as=jnp.bfloat16):
    drawn = jax.random.normal(stream_key, shape, jnp.float32) * deviation
    return jnp.minimum(jnp.maximum(drawn, -reach), reach).astype(held_as)


def setup_inputs(seed: int = 0) -> dict:
    keys = jax.random.split(jax.random.key(seed), 7)
    tokens = draw_tokens(jax.random.fold_in(keys[6], 71), 0)
    projection = draw_projection(jax.random.fold_in(keys[6], 71), 0)
    norm_gain = draw_norm_gain(jax.random.fold_in(keys[6], 71), 0)
    modulation = gaussian(keys[3], (LEVELS, 2, D), 0.5, 3.0, jnp.float32)
    levels = set_ends(jax.random.randint(keys[4], (FRAMES,), 0, LEVELS), jax.random.fold_in(keys[4], 1), 0, LEVELS - 1).astype(jnp.int32)
    frame_order = jax.random.permutation(keys[5], FRAMES).astype(jnp.int32)
    return dict(tokens=tokens, projection=projection, norm_gain=norm_gain, modulation=modulation, levels=levels, frame_order=frame_order)


LOWEST = -1e+30

def layer_input(tokens, levels, modulation):
    values = tokens.astype(jnp.float32)
    average = lax.optimization_barrier(jnp.mean(values, axis=-1, keepdims=True))
    centred = values - average
    spread = lax.optimization_barrier(jnp.mean(centred * centred, axis=-1, keepdims=True))
    normed = centred * lax.rsqrt(spread + 1e-06)
    onehot = (levels[:, None] == jnp.arange(LEVELS, dtype=jnp.int32)[None, :]).astype(jnp.float32)
    chosen = jnp.dot(onehot, modulation.reshape(LEVELS, 2 * D), precision=lax.Precision.HIGHEST)
    shifts = chosen[:, :D].reshape(-1, 1, 1, 1, D)
    scales = chosen[:, D:].reshape(-1, 1, 1, 1, D)
    return (normed * (1.0 + scales) + shifts).astype(jnp.bfloat16)

def root_norm(values, gains):
    return (values * lax.rsqrt(lax.optimization_barrier(jnp.mean(values * values, axis=-1, keepdims=True)) + 1e-06) * gains).astype(jnp.bfloat16)

def project_tokens(tokens, projection, norm_gain, modulation, levels):
    modulated = layer_input(tokens, levels, modulation)
    inner_width = projection.shape[1] // 3
    projected = jnp.dot(modulated.reshape(-1, D), projection, preferred_element_type=jnp.float32)
    queries = root_norm(projected[:, :inner_width], norm_gain[0])
    key_rows = root_norm(projected[:, inner_width:2 * inner_width], norm_gain[1])
    values = projected[:, 2 * inner_width:].astype(jnp.bfloat16)
    out_shape = tokens.shape[:-1] + (inner_width,)
    return (queries.reshape(out_shape), jnp.concatenate([key_rows.reshape(out_shape), values.reshape(out_shape)], axis=-1))

def reference(tokens, projection, norm_gain, modulation, levels, frame_order):
    queries, keys_values = project_tokens(tokens, projection, norm_gain, modulation, levels)
    frames = queries.shape[0]
    tile_total = queries.shape[1]
    tile_cols = tile_total // TROWS
    height = TROWS * TILE
    span_cols = tile_cols * TILE
    frame_kv = keys_values.reshape(frames, TROWS, tile_cols, TILE, TILE, 2 * QD).transpose(0, 1, 3, 2, 4, 5)
    frame_kv = frame_kv.reshape(frames, height, span_cols, 2 * QD)
    padded_kv = jnp.pad(frame_kv, ((0, 0), (PAD, PAD), (PAD, PAD), (0, 0)))
    row_ids = jnp.arange(height + 2 * PAD, dtype=jnp.int32)
    col_ids = jnp.arange(span_cols + 2 * PAD, dtype=jnp.int32)
    row_inside = (row_ids >= PAD) & (row_ids < PAD + height)
    col_inside = (col_ids >= PAD) & (col_ids < PAD + span_cols)
    inside = row_inside[:, None] & col_inside[None, :]
    window_side = TILE + 2 * PAD
    score_scale = 1.0 / math.sqrt(HD)
    anchor = jnp.zeros((), jnp.int32)

    def one_pair(pair_index):
        tile_index = pair_index // frames
        frame_index = pair_index % frames
        row_start = tile_index // tile_cols * TILE
        col_start = tile_index % tile_cols * TILE
        query_tile = lax.dynamic_slice(queries, (frame_index, tile_index, anchor, anchor, anchor), (1, 1, TILE, TILE, QD))
        query_tile = query_tile.reshape(TILE * TILE, HEADS, HD).astype(jnp.float32)
        window_kv = lax.dynamic_slice(padded_kv, (anchor, row_start, col_start, anchor), (frames, window_side, window_side, 2 * QD))
        window_kv = window_kv.reshape(frames, window_side * window_side, 2, HEADS, HD).astype(jnp.float32)
        window_inside = lax.dynamic_slice(inside, (row_start, col_start), (window_side, window_side)).reshape(window_side * window_side)
        own_order = lax.dynamic_index_in_dim(frame_order, frame_index, 0, keepdims=False)
        visible = frame_order <= own_order
        scores = jnp.einsum('qhd,gkhd->hqgk', query_tile, window_kv[:, :, 0]) * score_scale
        allowed = visible[None, None, :, None] & window_inside[None, None, None, :]
        maxima = lax.optimization_barrier(jnp.max(jnp.where(allowed, scores, LOWEST), axis=(2, 3), keepdims=True))
        exp_scores = jnp.where(allowed, jnp.exp(scores - maxima), 0.0)
        totals = lax.optimization_barrier(jnp.sum(exp_scores, axis=(2, 3)))
        rounded = lax.optimization_barrier(exp_scores.astype(jnp.bfloat16)).astype(jnp.float32)
        accumulated = jnp.einsum('hqgk,gkhd->qhd', rounded, window_kv[:, :, 1])
        result = accumulated / jnp.transpose(totals)[..., None]
        return result.astype(jnp.bfloat16).reshape(TILE, TILE, QD)
    results = lax.map(one_pair, jnp.arange(tile_total * frames, dtype=jnp.int32))
    return results.reshape(tile_total, frames, TILE, TILE, QD).transpose(1, 0, 2, 3, 4)
```

```python
import functools
import math

import jax
import jax.numpy as jnp
from jax import lax
from jax.experimental import pallas as pl
from jax.experimental.pallas import tpu as pltpu
from jax.sharding import PartitionSpec as P

D = 1536
HEADS = 6
HD = 128
TILE = 16
PAD = 2
TOKENS = TILE * TILE
QD = HEADS * HD
FRAMES = 32
CHIPS = 16
SLOTS = 8
RIM = 112
LOWEST = -1e30
LOG2E = math.log2(math.e)
SCALE = LOG2E / math.sqrt(HD)
AXES = ("tm", "ha")


def device_pairs(target):
    pairs = []
    for tm in range(CHIPS):
        for ha in range(8):
            goal = target(tm, ha // 2, ha % 2)
            if goal is not None:
                pairs.append((tm * 8 + ha, goal[0] * 8 + goal[1] * 2 + goal[2]))
    return pairs


def project_kernel(info, tokens, weights, gains, modulation, own, away, inputs):
    part = pl.program_id(0)
    step = pl.program_id(1)

    @pl.when(part == 0)
    def _():
        values = tokens[0].astype(jnp.float32)
        average = jnp.mean(values, axis=-1, keepdims=True)
        centred = values - average
        spread = jnp.mean(centred * centred, axis=-1, keepdims=True)
        normed = centred * lax.rsqrt(spread + 1e-06)
        shift = modulation[0, 0:1, :]
        scale = modulation[0, 1:2, :]
        inputs[step] = (normed * (1.0 + scale) + shift).astype(jnp.bfloat16)

    raw = jnp.dot(inputs[step], weights[...], preferred_element_type=jnp.float32)

    def put(result):
        result = result.astype(jnp.bfloat16)

        @pl.when(step == 0)
        def _():
            for head in range(HEADS):
                away[head, 0] = result[:, head * HD : (head + 1) * HD]

        @pl.when(step == 1)
        def _():
            for head in range(HEADS):
                own[head, 0] = result[:, head * HD : (head + 1) * HD]

    @pl.when(part < 2)
    def _():
        row = jnp.where(part == 0, gains[0:1, :], gains[1:2, :])
        put(raw * lax.rsqrt(jnp.mean(raw * raw, axis=-1, keepdims=True) + 1e-06) * row)

    @pl.when(part == 2)
    def _():
        put(raw)


def project(tokens, projection, norm_gain, modulation, levels, core):
    info = jnp.stack([core, levels[0], levels[1]])

    def frame(step, info):
        return info[0] + 1 - step - 2 * info[0] * (1 - step)

    return pl.pallas_call(
        project_kernel,
        grid_spec=pltpu.PrefetchScalarGridSpec(
            num_scalar_prefetch=1,
            grid=(3, 2),
            in_specs=[
                pl.BlockSpec((1, TOKENS, D), lambda p, s, info: (jnp.where(p == 0, frame(s, info), frame(1, info)), 0, 0)),
                pl.BlockSpec((D, QD), lambda p, s, info: (0, p)),
                pl.BlockSpec((2, QD), lambda p, s, info: (0, 0)),
                pl.BlockSpec((1, 2, D), lambda p, s, info: (info[1 + frame(s, info)], 0, 0)),
            ],
            out_specs=[
                pl.BlockSpec((SLOTS, 1, TOKENS, HD), lambda p, s, info: (info[0], p, 0, 0)),
                pl.BlockSpec((SLOTS, 1, TOKENS, HD), lambda p, s, info: (0, p, 0, 0)),
            ],
            scratch_shapes=[pltpu.VMEM((2, TOKENS, D), jnp.bfloat16)],
        ),
        out_shape=[
            jax.ShapeDtypeStruct((CHIPS, 3, TOKENS, HD), jnp.bfloat16),
            jax.ShapeDtypeStruct((SLOTS, 3, TOKENS, HD), jnp.bfloat16),
        ],
        compiler_params=pltpu.CompilerParams(vmem_limit_bytes=48 * 1024 * 1024),
        name="project",
    )(info, tokens, projection, norm_gain, modulation)


def soft_step(query, keys, values, bias, state):
    top, total, mixed = state
    scores = lax.dot_general(query, keys, (((1,), (1,)), ((), ())), preferred_element_type=jnp.float32)
    if bias is not None:
        scores = scores + bias
    count = keys.shape[0]
    groups = count // HD
    highest = scores[:, :HD]
    for group in range(1, groups):
        highest = jnp.maximum(highest, scores[:, group * HD : (group + 1) * HD])
    highest = jnp.max(highest, axis=-1, keepdims=True) * SCALE
    newest = jnp.maximum(top, jnp.broadcast_to(highest, top.shape))
    rescale = jnp.exp2(top - newest)
    total = total * rescale
    pieces = []
    for group in range(groups):
        piece = jnp.exp2(scores[:, group * HD : (group + 1) * HD] * SCALE - newest)
        total = total + piece
        pieces.append(piece.astype(jnp.bfloat16))
    weights = jnp.concatenate(pieces, axis=1)
    mixed = mixed * rescale + jnp.dot(weights, values, preferred_element_type=jnp.float32)
    return newest, total, mixed


def sort_frames(info, near, far, near_at, keys, values, sem, size):
    def start(time, carry):
        slot = info[time]
        chip = slot // 2
        mine = slot % 2 == info[FRAMES]
        rows = pl.ds(pl.multiple_of(time * size, size), size)

        @pl.when(mine)
        def _():
            pltpu.make_async_copy(near.at[chip, near_at], keys.at[rows], sem.at[0]).start()
            pltpu.make_async_copy(near.at[chip, near_at + 1], values.at[rows], sem.at[1]).start()

        @pl.when(jnp.logical_not(mine))
        def _():
            pltpu.make_async_copy(far.at[chip, 0], keys.at[rows], sem.at[0]).start()
            pltpu.make_async_copy(far.at[chip, 1], values.at[rows], sem.at[1]).start()

        return carry

    lax.fori_loop(0, FRAMES, start, 0)
    pltpu.make_async_copy(keys, keys, sem.at[0]).wait()
    pltpu.make_async_copy(values, values, sem.at[1]).wait()


WIDE = 1024


def main_kernel(info, query, near, far, top_out, total_out, mixed_out, keys, values, sem):
    index = pl.program_id(0)

    @pl.when(index == 0)
    def _():
        sort_frames(info, near, far, 1, keys, values, sem, TOKENS)

    frames = info[FRAMES + 1 + index]
    mine = query[0, 0]
    top_out[0] = jnp.full((TOKENS, HD), LOWEST, jnp.float32)
    total_out[0] = jnp.zeros((TOKENS, HD), jnp.float32)
    mixed_out[0] = jnp.zeros((TOKENS, HD), jnp.float32)

    def run(first, count):
        rows = pl.ds(pl.multiple_of(first, TOKENS), count)
        state = (top_out[0], total_out[0], mixed_out[0])
        top, total, mixed = soft_step(mine, keys[rows], values[rows], None, state)
        top_out[0] = top
        total_out[0] = total
        mixed_out[0] = mixed

    per = WIDE // TOKENS
    whole = frames // per

    def body(step, carry):
        run(step * WIDE, WIDE)
        return carry

    lax.fori_loop(0, whole, body, 0)

    def tail(step, carry):
        run(whole * WIDE + step * TOKENS, TOKENS)
        return carry

    lax.fori_loop(0, frames - whole * per, tail, 0)


RIM_WIDE = 512


def rim_kernel(info, query, near, far, bias, top_in, total_in, mixed_in, out, keys, values, sem):
    index = pl.program_id(0)

    @pl.when(index == 0)
    def _():
        sort_frames(info, near, far, 0, keys, values, sem, RIM)

    visible = info[FRAMES + 1 + index] * RIM
    mine = query[0, 0]

    def body(step, state):
        rows = pl.ds(pl.multiple_of(step * RIM_WIDE, RIM_WIDE), RIM_WIDE)
        place = lax.broadcasted_iota(jnp.int32, (1, RIM_WIDE), 1) + step * RIM_WIDE
        row_bias = jnp.where(place < visible, bias[0:1, rows], LOWEST)
        return soft_step(mine, keys[rows], values[rows], row_bias, state)

    steps = (visible + RIM_WIDE - 1) // RIM_WIDE
    top, total, mixed = lax.fori_loop(0, steps, body, (top_in[0], total_in[0], mixed_in[0]))
    out[0] = (mixed / jnp.sum(total, axis=-1, keepdims=True)).astype(jnp.bfloat16)


def attend_main(info, received, far):
    state_spec = pl.BlockSpec((1, TOKENS, HD), lambda i, info: (i, 0, 0))
    state_shape = jax.ShapeDtypeStruct((CHIPS, TOKENS, HD), jnp.float32)
    return pl.pallas_call(
        main_kernel,
        grid_spec=pltpu.PrefetchScalarGridSpec(
            num_scalar_prefetch=1,
            grid=(CHIPS,),
            in_specs=[
                pl.BlockSpec((1, 1, TOKENS, HD), lambda i, info: (i, 0, 0, 0)),
                pl.BlockSpec(memory_space=pl.ANY),
                pl.BlockSpec(memory_space=pl.ANY),
            ],
            out_specs=[state_spec] * 3,
            scratch_shapes=[
                pltpu.VMEM((FRAMES * TOKENS, HD), jnp.bfloat16),
                pltpu.VMEM((FRAMES * TOKENS, HD), jnp.bfloat16),
                pltpu.SemaphoreType.DMA((2,)),
            ],
        ),
        out_shape=[state_shape] * 3,
        compiler_params=pltpu.CompilerParams(vmem_limit_bytes=48 * 1024 * 1024),
        name="attend_main",
    )(info, received, received, far)


def attend_rims(info, received, near, far, bias, state):
    state_spec = pl.BlockSpec((1, TOKENS, HD), lambda i, info: (i, 0, 0))
    return pl.pallas_call(
        rim_kernel,
        grid_spec=pltpu.PrefetchScalarGridSpec(
            num_scalar_prefetch=1,
            grid=(CHIPS,),
            in_specs=[
                pl.BlockSpec((1, 1, TOKENS, HD), lambda i, info: (i, 0, 0, 0)),
                pl.BlockSpec(memory_space=pl.ANY),
                pl.BlockSpec(memory_space=pl.ANY),
                pl.BlockSpec((1, FRAMES * RIM), lambda i, info: (0, 0)),
            ]
            + [state_spec] * 3,
            out_specs=state_spec,
            scratch_shapes=[
                pltpu.VMEM((FRAMES * RIM, HD), jnp.bfloat16),
                pltpu.VMEM((FRAMES * RIM, HD), jnp.bfloat16),
                pltpu.SemaphoreType.DMA((2,)),
            ],
        ),
        out_shape=jax.ShapeDtypeStruct((CHIPS, TOKENS, HD), jnp.bfloat16),
        compiler_params=pltpu.CompilerParams(vmem_limit_bytes=48 * 1024 * 1024),
        name="attend_rims",
    )(info, received, near, far, bias, *state)


def swap_cores(value):
    return lax.ppermute(value, "ha", [(i, i ^ 1) for i in range(8)])


def to_right(tm, z, core):
    if tm < SLOTS:
        return (tm + SLOTS, z, core)
    return (tm - SLOTS, z + 1, core) if z % 2 == 0 else None


def to_left(tm, z, core):
    if tm >= SLOTS:
        return (tm - SLOTS, z, core)
    return (tm + SLOTS, z - 1, core) if z % 2 == 1 else None


def rim_keys(main, depth, kind):
    left = lax.ppermute(main[:, :, :, TILE - PAD :], AXES, device_pairs(to_right))
    right = lax.ppermute(main[:, :, :, :PAD], AXES, device_pairs(to_left))

    def rows(first):
        span = slice(first, first + PAD)
        return jnp.concatenate([left[:, :, span], main[:, :, span], right[:, :, span]], axis=3)

    edge = jnp.where(depth < 2, rows(TILE - PAD), rows(0))
    across = lax.ppermute(edge, "ha", [(i, i ^ 4) for i in range(8)])
    flat = [piece.reshape(CHIPS, 2, -1, HD) for piece in (left, right, across)]
    spare = jnp.zeros((CHIPS, 2, RIM - sum(p.shape[2] for p in flat), HD), jnp.bfloat16)
    return jnp.concatenate(flat + [spare], axis=2)


def rim_bias(column):
    place = jnp.arange(RIM, dtype=jnp.int32)
    across = (place - 64) % 20
    is_across = (place >= 64) & (place < 104)
    is_left = (place < 32) | (is_across & (across < PAD))
    is_right = ((place >= 32) & (place < 64)) | (is_across & (across >= TILE + PAD))
    valid = (place < 104) & ~(is_left & (column == 0)) & ~(is_right & (column == 3))
    return jnp.tile(jnp.where(valid, 0.0, LOWEST).astype(jnp.float32), FRAMES)[None]


def shards(tokens, projection, norm_gain, modulation, levels, frame_order):
    chip = lax.axis_index("tm")
    place = lax.axis_index("ha")
    depth = place // 2
    core = place % 2
    sending, away = project(tokens.reshape(2, TOKENS, D), projection, norm_gain, modulation, levels, core)
    other = swap_cores(away)
    sending = lax.dynamic_update_slice_in_dim(sending, other, (1 - core) * SLOTS, 0)
    received = lax.all_to_all(sending, "tm", 0, 0, tiled=True)
    far = swap_cores(received[:, 1:])

    slots = jnp.zeros((FRAMES,), jnp.int32).at[frame_order].set(jnp.arange(FRAMES, dtype=jnp.int32))
    own_order = lax.dynamic_index_in_dim(frame_order.reshape(CHIPS, 2), core, 1, keepdims=False)
    info = jnp.concatenate([slots, core[None], own_order + 1])

    state = attend_main(info, received, far)
    rims = rim_keys(received[:, 1:].reshape(CHIPS, 2, TILE, TILE, HD), depth, chip // SLOTS)
    far_rims = swap_cores(rims)
    bias = rim_bias((2 * depth + chip // SLOTS) % 4)
    mixed = attend_rims(info, received, rims, far_rims, bias, state)

    back = lax.all_to_all(mixed, "tm", 0, 0, tiled=True)
    stay = lax.dynamic_slice_in_dim(back, core * SLOTS, HEADS, 0)
    leave = lax.dynamic_slice_in_dim(back, (1 - core) * SLOTS, HEADS, 0)
    come = swap_cores(leave)
    both = jnp.where(core == 0, jnp.stack([stay, come]), jnp.stack([come, stay]))
    return both.transpose(0, 2, 1, 3).reshape(2, 1, TILE, TILE, QD)


def solution(mesh):
    in_specs = (P("tm", "ha", None, None, None), P(), P(), P(), P("tm"), P())
    out_specs = P("tm", "ha", None, None, None)
    return jax.shard_map(shards, mesh=mesh, in_specs=in_specs, out_specs=out_specs, check_vma=False)
```

```python
import functools
import math

import jax
import jax.numpy as jnp
from jax import lax
from jax.experimental import pallas as pl
from jax.experimental.pallas import tpu as pltpu
from jax.sharding import PartitionSpec as P

D = 1536
HEADS = 6
HD = 128
TILE = 16
PAD = 2
TOKENS = TILE * TILE
QD = HEADS * HD
FRAMES = 32
CHIPS = 16
SLOTS = 8
RIM = 112
LOWEST = -1e30
LOG2E = math.log2(math.e)
SCALE = LOG2E / math.sqrt(HD)
AXES = ("tm", "ha")


def device_pairs(target):
    pairs = []
    for tm in range(CHIPS):
        for ha in range(8):
            goal = target(tm, ha // 2, ha % 2)
            if goal is not None:
                pairs.append((tm * 8 + ha, goal[0] * 8 + goal[1] * 2 + goal[2]))
    return pairs


def project_kernel(info, tokens, weights, gains, modulation, own, away, inputs):
    part = pl.program_id(0)
    step = pl.program_id(1)

    @pl.when(part == 0)
    def _():
        values = tokens[0].astype(jnp.float32)
        average = jnp.mean(values, axis=-1, keepdims=True)
        centred = values - average
        spread = jnp.mean(centred * centred, axis=-1, keepdims=True)
        normed = centred * lax.rsqrt(spread + 1e-06)
        shift = modulation[0, 0:1, :]
        scale = modulation[0, 1:2, :]
        inputs[step] = (normed * (1.0 + scale) + shift).astype(jnp.bfloat16)

    raw = jnp.dot(inputs[step], weights[...], preferred_element_type=jnp.float32)

    def put(result):
        result = result.astype(jnp.bfloat16)

        @pl.when(step == 0)
        def _():
            for head in range(HEADS):
                away[head, 0] = result[:, head * HD : (head + 1) * HD]

        @pl.when(step == 1)
        def _():
            for head in range(HEADS):
                own[head, 0] = result[:, head * HD : (head + 1) * HD]

    @pl.when(part < 2)
    def _():
        row = jnp.where(part == 0, gains[0:1, :], gains[1:2, :])
        put(raw * lax.rsqrt(jnp.mean(raw * raw, axis=-1, keepdims=True) + 1e-06) * row)

    @pl.when(part == 2)
    def _():
        put(raw)


def project(tokens, projection, norm_gain, modulation, levels, core):
    info = jnp.stack([core, levels[0], levels[1]])

    def frame(step, info):
        return info[0] + 1 - step - 2 * info[0] * (1 - step)

    return pl.pallas_call(
        project_kernel,
        grid_spec=pltpu.PrefetchScalarGridSpec(
            num_scalar_prefetch=1,
            grid=(3, 2),
            in_specs=[
                pl.BlockSpec((1, TOKENS, D), lambda p, s, info: (jnp.where(p == 0, frame(s, info), frame(1, info)), 0, 0)),
                pl.BlockSpec((D, QD), lambda p, s, info: (0, p)),
                pl.BlockSpec((2, QD), lambda p, s, info: (0, 0)),
                pl.BlockSpec((1, 2, D), lambda p, s, info: (info[1 + frame(s, info)], 0, 0)),
            ],
            out_specs=[
                pl.BlockSpec((SLOTS, 1, TOKENS, HD), lambda p, s, info: (info[0], p, 0, 0)),
                pl.BlockSpec((SLOTS, 1, TOKENS, HD), lambda p, s, info: (0, p, 0, 0)),
            ],
            scratch_shapes=[pltpu.VMEM((2, TOKENS, D), jnp.bfloat16)],
        ),
        out_shape=[
            jax.ShapeDtypeStruct((CHIPS, 3, TOKENS, HD), jnp.bfloat16),
            jax.ShapeDtypeStruct((SLOTS, 3, TOKENS, HD), jnp.bfloat16),
        ],
        compiler_params=pltpu.CompilerParams(vmem_limit_bytes=48 * 1024 * 1024),
        name="project",
    )(info, tokens, projection, norm_gain, modulation)


STREAMS = 2
EACH = CHIPS // STREAMS
WIDE = 512
LIMIT = EACH * (FRAMES * TOKENS // WIDE)
ROWS = STREAMS * (EACH + 1)


def plan(order, core, size, slots, chips, pick, block, left):
    for slot in range(FRAMES):
        slots[order[slot]] = slot

    def clear(step, carry):
        for stream in range(STREAMS):
            pick[stream, step] = EACH
            block[stream, step] = 0
            left[stream, step] = WIDE
        return carry

    def visit(turn, carry):
        place = carry[0]
        time = FRAMES - 1 - turn
        slot = slots[time]
        mine = slot % 2 == core
        lane = place % (2 * STREAMS)
        stream = jnp.where(lane < STREAMS, lane, 2 * STREAMS - 1 - lane)
        row = place // STREAMS
        rows = (time + 1) * size
        count = jnp.where(mine, (rows + WIDE - 1) // WIDE, 0)
        used = carry[1]
        for other in range(1, STREAMS):
            used = jnp.where(stream == other, carry[1 + other], used)

        @pl.when(mine)
        def _():
            chips[row * STREAMS + stream] = slot // 2

        def fill(step, inner):
            pick[stream, used + step] = row
            block[stream, used + step] = step
            left[stream, used + step] = rows - step * WIDE
            return inner

        lax.fori_loop(0, count, fill, 0)
        grown = tuple(carry[1 + s] + jnp.where(stream == s, count, 0) for s in range(STREAMS))
        return (place + jnp.where(mine, 1, 0),) + grown

    zero = jnp.int32(0)
    lax.fori_loop(0, LIMIT + 2, clear, 0)
    totals = lax.fori_loop(0, FRAMES, visit, (zero,) + (zero,) * STREAMS)[1:]
    return functools.reduce(jnp.maximum, totals)


def fold(values, combine):
    return combine(values.reshape(values.shape[0] // 8, 8, values.shape[1]), axis=0)


def sweep(trip, scored, queries, keys, values, tops, totals, mixes, pick, block, left, raws):
    def spots_of(step):
        spots = []
        for stream in range(STREAMS):
            row = pick[stream, step] * STREAMS + stream
            first = pl.multiple_of(block[stream, step] * WIDE, WIDE)
            spots.append((row, pl.ds(first, WIDE)))
        return spots

    def ask(step, slot):
        for stream, (row, rows) in enumerate(spots_of(step)):
            raws[slot][stream][...] = jnp.dot(keys[rows], queries[row], preferred_element_type=jnp.float32)

    def answer(step, slot):
        spots = spots_of(step)
        weighed = []
        for stream, (row, rows) in enumerate(spots):
            scores = scored(raws[slot][stream][...], rows, left[stream, step])
            highest = jnp.max(fold(scores, jnp.max), axis=0, keepdims=True) * SCALE
            top = tops[row]
            newest = jnp.maximum(top, highest)
            rescale = jnp.exp2(top - newest)
            weights = jnp.exp2(scores * SCALE - newest[0:1])
            total = totals[row] * rescale + fold(weights, jnp.sum)
            weighed.append((newest, total, rescale, weights.astype(jnp.bfloat16)))
        fresh = [jnp.dot(values[:, rows], weighed[stream][3], preferred_element_type=jnp.float32) for stream, (row, rows) in enumerate(spots)]
        mixed = [mixes[row] * weighed[stream][2][0:1] + fresh[stream] for stream, (row, rows) in enumerate(spots)]
        for stream, (row, rows) in enumerate(spots):
            tops[row] = weighed[stream][0]
            totals[row] = weighed[stream][1]
            mixes[row] = mixed[stream]

    def body(pair, carry):
        ask(2 * pair + 1, 1)
        answer(2 * pair, 0)
        ask(2 * pair + 2, 0)
        answer(2 * pair + 1, 1)
        return carry

    ask(0, 0)
    lax.fori_loop(0, (trip + 1) // 2, body, 0)


def gather_frames(order_slots, core, near, far, near_at, keys, staged, sem, size):
    def start(time, carry):
        slot = order_slots[time]
        chip = slot // 2
        mine = slot % 2 == core
        rows = pl.ds(pl.multiple_of(time * size, size), size)

        @pl.when(mine)
        def _():
            pltpu.make_async_copy(near.at[chip, near_at], keys.at[rows], sem.at[0]).start()
            pltpu.make_async_copy(near.at[chip, near_at + 1], staged.at[rows], sem.at[1]).start()

        @pl.when(jnp.logical_not(mine))
        def _():
            pltpu.make_async_copy(far.at[chip, 0], keys.at[rows], sem.at[0]).start()
            pltpu.make_async_copy(far.at[chip, 1], staged.at[rows], sem.at[1]).start()

        return carry

    lax.fori_loop(0, FRAMES, start, 0)


def turn_values(staged, values, total):
    def turn(step, carry):
        rows = pl.ds(pl.multiple_of(step * WIDE, WIDE), WIDE)
        values[:, rows] = staged[rows].T
        return carry

    lax.fori_loop(0, total // WIDE, turn, 0)


def turn_queries(chips, staged, queries):
    for place in range(CHIPS):
        queries[place] = staged[chips[place]].T


def main_kernel(info, near, far, tops, totals, mixes, queries, asked, keys, staged, values, slots, chips, pick, block, left, sem, *raws):
    core = info[FRAMES]
    trip = plan(info, core, TOKENS, slots, chips, pick, block, left)
    asking = pltpu.make_async_copy(near.at[:, 0], asked, sem.at[2])
    asking.start()
    gather_frames(slots, core, near, far, 1, keys, staged, sem, TOKENS)
    tops[...] = jnp.full(tops.shape, LOWEST, jnp.float32)
    totals[...] = jnp.zeros(totals.shape, jnp.float32)
    mixes[...] = jnp.zeros(mixes.shape, jnp.float32)
    queries[pl.ds(CHIPS, STREAMS)] = jnp.zeros((STREAMS, HD, TOKENS), jnp.bfloat16)
    asking.wait()
    turn_queries(chips, asked, queries)
    pltpu.make_async_copy(keys, keys, sem.at[0]).wait()
    pltpu.make_async_copy(staged, staged, sem.at[1]).wait()
    turn_values(staged, values, FRAMES * TOKENS)

    def scored(raw, rows, remain):
        half = WIDE // 2
        return jnp.concatenate([raw[:half], raw[half:] + jnp.where(remain < WIDE, LOWEST, 0.0)], axis=0)

    sweep(trip, scored, queries, keys, values, tops, totals, mixes, pick, block, left, (raws[:STREAMS], raws[STREAMS:]))


def rim_kernel(info, near, far, bias, queries, tops_in, totals_in, mixes_in, out, tops, totals, mixes, keys, staged, values, slots, chips, pick, block, left, sem, *raws):
    core = info[FRAMES]
    trip = plan(info, core, RIM, slots, chips, pick, block, left)
    gather_frames(slots, core, near, far, 0, keys, staged, sem, RIM)
    tops[...] = tops_in[...]
    totals[...] = totals_in[...]
    mixes[...] = mixes_in[...]
    pltpu.make_async_copy(keys, keys, sem.at[0]).wait()
    pltpu.make_async_copy(staged, staged, sem.at[1]).wait()
    turn_values(staged, values, FRAMES * RIM)

    def scored(raw, rows, remain):
        place = lax.broadcasted_iota(jnp.int32, (WIDE, HD), 0)
        added = jnp.where(place < remain, bias[rows], LOWEST)
        return jnp.concatenate([raw[:, :HD] + added, raw[:, HD:] + added], axis=1)

    sweep(trip, scored, queries, keys, values, tops, totals, mixes, pick, block, left, (raws[:STREAMS], raws[STREAMS:]))
    for place in range(CHIPS):
        whole = jnp.sum(totals[place], axis=0, keepdims=True)
        out[chips[place]] = (mixes[place] / whole).T.astype(jnp.bfloat16)


STATE = [
    jax.ShapeDtypeStruct((ROWS, 8, TOKENS), jnp.float32),
    jax.ShapeDtypeStruct((ROWS, 8, TOKENS), jnp.float32),
    jax.ShapeDtypeStruct((ROWS, HD, TOKENS), jnp.float32),
]


def key_scratch(total):
    return [
        pltpu.VMEM((total, HD), jnp.bfloat16),
        pltpu.VMEM((total, HD), jnp.bfloat16),
        pltpu.VMEM((HD, total), jnp.bfloat16),
        pltpu.SMEM((FRAMES,), jnp.int32),
        pltpu.SMEM((CHIPS,), jnp.int32),
        pltpu.SMEM((STREAMS, LIMIT + 2), jnp.int32),
        pltpu.SMEM((STREAMS, LIMIT + 2), jnp.int32),
        pltpu.SMEM((STREAMS, LIMIT + 2), jnp.int32),
        pltpu.SemaphoreType.DMA((3,)),
    ] + [pltpu.VMEM((WIDE, TOKENS), jnp.float32)] * (2 * STREAMS)


def whole(shape):
    return pl.BlockSpec(shape, lambda i, info: (0,) * len(shape))


def attend_main(info, received, far):
    shapes = STATE + [jax.ShapeDtypeStruct((ROWS, HD, TOKENS), jnp.bfloat16)]
    return pl.pallas_call(
        main_kernel,
        grid_spec=pltpu.PrefetchScalarGridSpec(
            num_scalar_prefetch=1,
            grid=(1,),
            in_specs=[pl.BlockSpec(memory_space=pl.ANY), pl.BlockSpec(memory_space=pl.ANY)],
            out_specs=[whole(s.shape) for s in shapes],
            scratch_shapes=[pltpu.VMEM((CHIPS, TOKENS, HD), jnp.bfloat16)] + key_scratch(FRAMES * TOKENS),
        ),
        out_shape=shapes,
        cost_estimate=pl.CostEstimate(flops=10**10, bytes_accessed=8 * 10**6, transcendentals=2 * 10**7),
        compiler_params=pltpu.CompilerParams(vmem_limit_bytes=48 * 1024 * 1024),
        name="attend_main",
    )(info, received, far)


def attend_rims(info, near, far, bias, state):
    shapes = [s.shape for s in STATE]
    out = (CHIPS, TOKENS, HD)
    return pl.pallas_call(
        rim_kernel,
        grid_spec=pltpu.PrefetchScalarGridSpec(
            num_scalar_prefetch=1,
            grid=(1,),
            in_specs=[pl.BlockSpec(memory_space=pl.ANY), pl.BlockSpec(memory_space=pl.ANY), whole(bias.shape)]
            + [whole((ROWS, HD, TOKENS))]
            + [whole(s) for s in shapes],
            out_specs=whole(out),
            scratch_shapes=[pltpu.VMEM(s.shape, s.dtype) for s in STATE] + key_scratch(FRAMES * RIM),
        ),
        out_shape=jax.ShapeDtypeStruct(out, jnp.bfloat16),
        cost_estimate=pl.CostEstimate(flops=4 * 10**9, bytes_accessed=8 * 10**6, transcendentals=10**7),
        compiler_params=pltpu.CompilerParams(vmem_limit_bytes=48 * 1024 * 1024),
        name="attend_rims",
    )(info, near, far, bias, state[3], *state[:3])


def swap_cores(value):
    return lax.ppermute(value, "ha", [(i, i ^ 1) for i in range(8)])


def to_right(tm, z, core):
    if tm < SLOTS:
        return (tm + SLOTS, z, core)
    return (tm - SLOTS, z + 1, core) if z % 2 == 0 else None


def to_left(tm, z, core):
    if tm >= SLOTS:
        return (tm - SLOTS, z, core)
    return (tm + SLOTS, z - 1, core) if z % 2 == 1 else None


def across(step):
    def target(tm, z, core):
        goal = step(tm, z, core)
        return None if goal is None else (goal[0], goal[1] ^ 2, core)

    return target


def rim_pieces(main, depth):
    upper = depth < 2
    edge = jnp.where(upper, main[:, :, TILE - PAD :], main[:, :, :PAD])
    return [
        lax.ppermute(main[:, :, :, TILE - PAD :], AXES, device_pairs(to_right)),
        lax.ppermute(main[:, :, :, :PAD], AXES, device_pairs(to_left)),
        lax.ppermute(edge, "ha", [(i, i ^ 4) for i in range(8)]),
        lax.ppermute(edge[:, :, :, TILE - PAD :], AXES, device_pairs(across(to_right))),
        lax.ppermute(edge[:, :, :, :PAD], AXES, device_pairs(across(to_left))),
    ]


def rim_keys(pieces):
    flat = [piece.reshape(CHIPS, 2, -1, HD) for piece in pieces]
    spare = jnp.zeros((CHIPS, 2, RIM - sum(p.shape[2] for p in flat), HD), jnp.bfloat16)
    return jnp.concatenate(flat + [spare], axis=2)


def rim_bias(column):
    place = jnp.arange(RIM, dtype=jnp.int32)
    is_left = (place < 32) | ((place >= 96) & (place < 100))
    is_right = ((place >= 32) & (place < 64)) | ((place >= 100) & (place < 104))
    valid = (place < 104) & ~(is_left & (column == 0)) & ~(is_right & (column == 3))
    column_of = jnp.tile(jnp.where(valid, 0.0, LOWEST).astype(jnp.float32), FRAMES)
    return jnp.broadcast_to(column_of[:, None], (FRAMES * RIM, HD))


def shards(tokens, projection, norm_gain, modulation, levels, frame_order):
    chip = lax.axis_index("tm")
    place = lax.axis_index("ha")
    depth = place // 2
    core = place % 2
    sending, away = project(tokens.reshape(2, TOKENS, D), projection, norm_gain, modulation, levels, core)
    other = swap_cores(away)
    sending = lax.dynamic_update_slice_in_dim(sending, other, (1 - core) * SLOTS, 0)
    received = lax.all_to_all(sending, "tm", 0, 0, tiled=True)
    far = swap_cores(received[:, 1:])

    info = jnp.concatenate([frame_order, core[None]])
    pieces = rim_pieces(received[:, 1:].reshape(CHIPS, 2, TILE, TILE, HD), depth)
    state = attend_main(info, received, far)
    pieces, top = lax.optimization_barrier((pieces, state[0]))
    state = [top, *state[1:]]
    rims = rim_keys(pieces)
    far_rims = swap_cores(rims)
    bias = rim_bias((2 * depth + chip // SLOTS) % 4)
    mixed = attend_rims(info, rims, far_rims, bias, state)

    back = lax.all_to_all(mixed, "tm", 0, 0, tiled=True)
    stay = lax.dynamic_slice_in_dim(back, core * SLOTS, HEADS, 0)
    leave = lax.dynamic_slice_in_dim(back, (1 - core) * SLOTS, HEADS, 0)
    come = swap_cores(leave)
    both = jnp.where(core == 0, jnp.stack([stay, come]), jnp.stack([come, stay]))
    return both.transpose(0, 2, 1, 3).reshape(2, 1, TILE, TILE, QD)


def solution(mesh):
    in_specs = (P("tm", "ha", None, None, None), P(), P(), P(), P("tm"), P())
    out_specs = P("tm", "ha", None, None, None)
    return jax.shard_map(shards, mesh=mesh, in_specs=in_specs, out_specs=out_specs, check_vma=False)
```

```python
import functools
import math

import jax
import jax.numpy as jnp
from jax import lax
from jax.experimental import pallas as pl
from jax.experimental.pallas import tpu as pltpu
from jax.sharding import PartitionSpec as P

D = 1536
HEADS = 6
HD = 128
TILE = 16
PAD = 2
TOKENS = TILE * TILE
QD = HEADS * HD
FRAMES = 32
CHIPS = 16
SLOTS = 8
RIM = 112
LENGTH = 3 * TOKENS + 2 * RIM
LOWEST = -1e30
LOG2E = math.log2(math.e)
SCALE = LOG2E / math.sqrt(HD)
AXES = ("tm", "ha")


def project_kernel(info, tokens, weights, gains, first, second, own, away, inputs):
    part = pl.program_id(0)
    core = info[0]

    @pl.when(part == 0)
    def _():
        for turn in range(2):
            frame = 1 - core if turn == 0 else core
            values = tokens[frame].astype(jnp.float32)
            average = jnp.mean(values, axis=-1, keepdims=True)
            centred = values - average
            spread = jnp.mean(centred * centred, axis=-1, keepdims=True)
            normed = centred * lax.rsqrt(spread + 1e-06)
            shift = jnp.where(frame == 0, first[0, 0:1, :], second[0, 0:1, :])
            scale = jnp.where(frame == 0, first[0, 1:2, :], second[0, 1:2, :])
            inputs[pl.ds(turn * TOKENS, TOKENS)] = (normed * (1.0 + scale) + shift).astype(jnp.bfloat16)

    raw = jnp.dot(inputs[...], weights[...], preferred_element_type=jnp.float32)

    def put(result):
        result = result.astype(jnp.bfloat16)
        for head in range(HEADS):
            columns = slice(head * HD, (head + 1) * HD)
            away[head] = result[:TOKENS, columns]
            own[head] = result[TOKENS:, columns]

    @pl.when(part < 2)
    def _():
        row = jnp.where(part == 0, gains[0:1, :], gains[1:2, :])
        put(raw * lax.rsqrt(jnp.mean(raw * raw, axis=-1, keepdims=True) + 1e-06) * row)

    @pl.when(part == 2)
    def _():
        put(raw)


def project(tokens, projection, norm_gain, modulation, levels, core):
    info = jnp.concatenate([core[None], levels])
    return pl.pallas_call(
        project_kernel,
        grid_spec=pltpu.PrefetchScalarGridSpec(
            num_scalar_prefetch=1,
            grid=(3,),
            in_specs=[
                pl.BlockSpec((2, TOKENS, D), lambda p, info: (0, 0, 0)),
                pl.BlockSpec((D, QD), lambda p, info: (0, p)),
                pl.BlockSpec((2, QD), lambda p, info: (0, 0)),
                pl.BlockSpec((1, 2, D), lambda p, info: (info[1], 0, 0)),
                pl.BlockSpec((1, 2, D), lambda p, info: (info[2], 0, 0)),
            ],
            out_specs=[
                pl.BlockSpec((SLOTS, TOKENS, HD), lambda p, info: (info[0], p, 0)),
                pl.BlockSpec((SLOTS, TOKENS, HD), lambda p, info: (0, p, 0)),
            ],
            scratch_shapes=[pltpu.VMEM((2 * TOKENS, D), jnp.bfloat16)],
        ),
        out_shape=[
            jax.ShapeDtypeStruct((CHIPS, LENGTH, HD), jnp.bfloat16),
            jax.ShapeDtypeStruct((SLOTS, 3 * TOKENS, HD), jnp.bfloat16),
        ],
        compiler_params=pltpu.CompilerParams(vmem_limit_bytes=48 * 1024 * 1024),
        name="project",
    )(info, tokens, projection, norm_gain, modulation, modulation)


STREAMS = 2
EACH = CHIPS // STREAMS
WIDE = 512
LIMIT = EACH * (FRAMES * TOKENS // WIDE)
ROWS = STREAMS * (EACH + 1)


def plan(core, size, slots, chips, pick, block, left):
    def visit(turn, carry):
        place = carry[0]
        time = FRAMES - 1 - turn
        slot = slots[time]
        mine = slot % 2 == core
        lane = place % (2 * STREAMS)
        stream = jnp.where(lane < STREAMS, lane, 2 * STREAMS - 1 - lane)
        row = place // STREAMS
        rows = (time + 1) * size
        count = jnp.where(mine, (rows + WIDE - 1) // WIDE, 0)
        used = carry[1]
        for other in range(1, STREAMS):
            used = jnp.where(stream == other, carry[1 + other], used)

        @pl.when(mine)
        def _():
            chips[row * STREAMS + stream] = slot // 2

        def fill(step, inner):
            pick[stream, used + step] = row
            block[stream, used + step] = step
            left[stream, used + step] = rows - step * WIDE
            return inner

        lax.fori_loop(0, count, fill, 0)
        grown = tuple(carry[1 + s] + jnp.where(stream == s, count, 0) for s in range(STREAMS))
        return (place + jnp.where(mine, 1, 0),) + grown

    zero = jnp.int32(0)
    totals = lax.fori_loop(0, FRAMES, visit, (zero,) + (zero,) * STREAMS)[1:]
    trip = functools.reduce(jnp.maximum, totals)
    for stream in range(STREAMS):

        def clear(step, carry):
            pick[stream, step] = EACH
            block[stream, step] = 0
            left[stream, step] = WIDE
            return carry

        lax.fori_loop(totals[stream], trip + 2, clear, 0)
    return trip


def fold(values, combine):
    return combine(values.reshape(values.shape[0] // 8, 8, values.shape[1]), axis=0)


def sweep(trip, scored, queries, keys, values, tops, totals, mixes, pick, block, left, raws):
    def spots_of(step):
        spots = []
        for stream in range(STREAMS):
            row = pick[stream, step] * STREAMS + stream
            first = pl.multiple_of(block[stream, step] * WIDE, WIDE)
            spots.append((row, pl.ds(first, WIDE)))
        return spots

    def ask(step, slot):
        for stream, (row, rows) in enumerate(spots_of(step)):
            raws[slot][stream][...] = jnp.dot(keys[rows], queries[row], preferred_element_type=jnp.float32)

    def answer(step, slot):
        spots = spots_of(step)
        weighed = []
        for stream, (row, rows) in enumerate(spots):
            scores = scored(raws[slot][stream][...], rows, left[stream, step])
            highest = jnp.max(fold(scores, jnp.max), axis=0, keepdims=True) * SCALE
            top = tops[row]
            newest = jnp.maximum(top, highest)
            rescale = jnp.exp2(top - newest)
            weights = jnp.exp2(scores * SCALE - newest[0:1])
            total = totals[row] * rescale + fold(weights, jnp.sum)
            weighed.append((newest, total, rescale, weights.astype(jnp.bfloat16)))
        fresh = [jnp.dot(values[:, rows], weighed[stream][3], preferred_element_type=jnp.float32) for stream, (row, rows) in enumerate(spots)]
        mixed = [mixes[row] * weighed[stream][2][0:1] + fresh[stream] for stream, (row, rows) in enumerate(spots)]
        for stream, (row, rows) in enumerate(spots):
            tops[row] = weighed[stream][0]
            totals[row] = weighed[stream][1]
            mixes[row] = mixed[stream]

    def body(pair, carry):
        ask(2 * pair + 1, 1)
        answer(2 * pair, 0)
        ask(2 * pair + 2, 0)
        answer(2 * pair + 1, 1)
        return carry

    ask(0, 0)
    lax.fori_loop(0, (trip + 1) // 2, body, 0)


def gather_frames(slots, core, near, far, moves, sem):
    def start(time, carry):
        slot = slots[time]
        chip = slot // 2
        mine = slot % 2 == core

        def copy(source):
            for number, (first, size, target) in enumerate(moves):
                rows = pl.ds(pl.multiple_of(time * size, size), size)
                pltpu.make_async_copy(source.at[chip, pl.ds(first, size)], target.at[rows], sem.at[number]).start()

        pl.when(mine)(lambda: copy(near))
        pl.when(jnp.logical_not(mine))(lambda: copy(far))
        return carry

    lax.fori_loop(0, FRAMES, start, 0)


def turn_values(staged, values, total):
    def turn(step, carry):
        rows = pl.ds(pl.multiple_of(step * WIDE, WIDE), WIDE)
        values[:, rows] = staged[rows].T
        return carry

    lax.fori_loop(0, total // WIDE, turn, 0)


def turn_queries(chips, staged, queries):
    for place in range(CHIPS):
        queries[place] = staged[chips[place]].T


def attend_kernel(info, near, far, bias, out, *scratch):
    tops, totals, mixes, asked, queries, keys, staged, values, rim_keys, rim_staged, rim_values, slots, chips = scratch[:13]
    lists, rim_lists, sem, raws = scratch[13:16], scratch[16:19], scratch[19], scratch[20:]
    raws = (raws[:STREAMS], raws[STREAMS:])
    core = info[FRAMES]
    for slot in range(FRAMES):
        slots[info[slot]] = slot
    asking = pltpu.make_async_copy(near.at[:, pl.ds(0, TOKENS)], asked, sem.at[4])
    asking.start()
    rim_at = 3 * TOKENS
    moves = (
        (TOKENS, TOKENS, keys),
        (2 * TOKENS, TOKENS, staged),
        (rim_at, RIM, rim_keys),
        (rim_at + RIM, RIM, rim_staged),
    )
    gather_frames(slots, core, near, far, moves, sem)
    trip = plan(core, TOKENS, slots, chips, *lists)
    rim_trip = plan(core, RIM, slots, chips, *rim_lists)
    tops[...] = jnp.full(tops.shape, LOWEST, jnp.float32)
    totals[...] = jnp.zeros(totals.shape, jnp.float32)
    mixes[...] = jnp.zeros(mixes.shape, jnp.float32)
    queries[pl.ds(CHIPS, STREAMS)] = jnp.zeros((STREAMS, HD, TOKENS), jnp.bfloat16)
    asking.wait()
    turn_queries(chips, asked, queries)
    for number, move in enumerate(moves):
        pltpu.make_async_copy(move[2], move[2], sem.at[number]).wait()
    turn_values(staged, values, FRAMES * TOKENS)
    turn_values(rim_staged, rim_values, FRAMES * RIM)

    def scored(raw, rows, remain):
        half = WIDE // 2
        return jnp.concatenate([raw[:half], raw[half:] + jnp.where(remain < WIDE, LOWEST, 0.0)], axis=0)

    sweep(trip, scored, queries, keys, values, tops, totals, mixes, *lists, raws)

    def rim_scored(raw, rows, remain):
        place = lax.broadcasted_iota(jnp.int32, (WIDE, HD), 0)
        added = jnp.where(place < remain, bias[rows], LOWEST)
        return jnp.concatenate([raw[:, :HD] + added, raw[:, HD:] + added], axis=1)

    sweep(rim_trip, rim_scored, queries, rim_keys, rim_values, tops, totals, mixes, *rim_lists, raws)
    for place in range(CHIPS):
        whole = jnp.sum(totals[place], axis=0, keepdims=True)
        out[chips[place]] = (mixes[place] / whole).T.astype(jnp.bfloat16)


def attend(info, near, far, bias):
    lists = [pltpu.SMEM((STREAMS, LIMIT + 2), jnp.int32)] * 3
    return pl.pallas_call(
        attend_kernel,
        grid_spec=pltpu.PrefetchScalarGridSpec(
            num_scalar_prefetch=1,
            grid=(1,),
            in_specs=[
                pl.BlockSpec(memory_space=pl.ANY),
                pl.BlockSpec(memory_space=pl.ANY),
                pl.BlockSpec(bias.shape, lambda i, info: (0, 0)),
            ],
            out_specs=pl.BlockSpec((CHIPS, TOKENS, HD), lambda i, info: (0, 0, 0)),
            scratch_shapes=[
                pltpu.VMEM((ROWS, 8, TOKENS), jnp.float32),
                pltpu.VMEM((ROWS, 8, TOKENS), jnp.float32),
                pltpu.VMEM((ROWS, HD, TOKENS), jnp.float32),
                pltpu.VMEM((CHIPS, TOKENS, HD), jnp.bfloat16),
                pltpu.VMEM((ROWS, HD, TOKENS), jnp.bfloat16),
                pltpu.VMEM((FRAMES * TOKENS, HD), jnp.bfloat16),
                pltpu.VMEM((FRAMES * TOKENS, HD), jnp.bfloat16),
                pltpu.VMEM((HD, FRAMES * TOKENS), jnp.bfloat16),
                pltpu.VMEM((FRAMES * RIM, HD), jnp.bfloat16),
                pltpu.VMEM((FRAMES * RIM, HD), jnp.bfloat16),
                pltpu.VMEM((HD, FRAMES * RIM), jnp.bfloat16),
                pltpu.SMEM((FRAMES,), jnp.int32),
                pltpu.SMEM((CHIPS,), jnp.int32),
            ]
            + lists
            + lists
            + [pltpu.SemaphoreType.DMA((5,))]
            + [pltpu.VMEM((WIDE, TOKENS), jnp.float32)] * (2 * STREAMS),
        ),
        out_shape=jax.ShapeDtypeStruct((CHIPS, TOKENS, HD), jnp.bfloat16),
        compiler_params=pltpu.CompilerParams(vmem_limit_bytes=48 * 1024 * 1024),
        name="attend",
    )(info, near, far, bias)


def swap_cores(value):
    return lax.ppermute(value, "ha", [(i, i ^ 1) for i in range(8)])


def swap_depth(value, bits):
    return lax.ppermute(value, "ha", [(i, i ^ (2 * bits)) for i in range(8)])


def rim_rows(pair, depth):
    even = depth % 2 == 0
    upper = depth < 2

    def edge(strip):
        return jnp.where(upper, strip[..., TILE - PAD :, :, :], strip[..., :PAD, :, :])

    sent = jnp.where(even, pair[1, :, :, :, TILE - PAD :], pair[0, :, :, :, :PAD])
    outer = swap_depth(sent, 1)
    above = swap_depth(edge(pair), 2)
    corner = swap_depth(edge(sent), 3)
    inner = (pair[1, :, :, :, :PAD], pair[0, :, :, :, TILE - PAD :])
    inner_corner = (above[1, :, :, :, :PAD], above[0, :, :, :, TILE - PAD :])
    spare = jnp.zeros((SLOTS, 2, RIM - 104, HD), jnp.bfloat16)

    def flat(piece):
        return piece.reshape(SLOTS, 2, -1, HD)

    both = []
    for tile in range(2):
        rows = [inner[tile], above[tile], inner_corner[tile], outer, corner]
        both.append(jnp.concatenate([flat(r) for r in rows] + [spare], axis=2))
    return jnp.concatenate(both, axis=0).reshape(CHIPS, 2 * RIM, HD)


def rim_bias(outer_valid):
    place = jnp.arange(RIM, dtype=jnp.int32)
    valid = (place < 68) | ((place < 104) & outer_valid)
    column_of = jnp.tile(jnp.where(valid, 0.0, LOWEST).astype(jnp.float32), FRAMES)
    return jnp.broadcast_to(column_of[:, None], (FRAMES * RIM, HD))


def shards(tokens, projection, norm_gain, modulation, levels, frame_order):
    chip = lax.axis_index("tm")
    place = lax.axis_index("ha")
    depth = place // 2
    core = place % 2
    sending, away = project(tokens.reshape(2, TOKENS, D), projection, norm_gain, modulation, levels, core)
    other = swap_cores(away)
    first = (1 - core) * SLOTS
    sending = lax.dynamic_update_slice(sending, other, (first, 0, 0))
    pair = sending[:, TOKENS : 3 * TOKENS].reshape(2, SLOTS, 2, TILE, TILE, HD)
    sending = lax.dynamic_update_slice(sending, rim_rows(pair, depth), (0, 3 * TOKENS, 0))
    received = lax.all_to_all(sending, "tm", 0, 0, tiled=True)
    far = swap_cores(received)

    info = jnp.concatenate([frame_order, core[None]])
    odd_tile = chip // SLOTS
    bias = rim_bias(depth % 2 != odd_tile)
    mixed = attend(info, received, far, bias)

    back = lax.all_to_all(mixed, "tm", 0, 0, tiled=True)
    stay = lax.dynamic_slice_in_dim(back, core * SLOTS, HEADS, 0)
    leave = lax.dynamic_slice_in_dim(back, (1 - core) * SLOTS, HEADS, 0)
    come = swap_cores(leave)
    both = jnp.where(core == 0, jnp.stack([stay, come]), jnp.stack([come, stay]))
    return both.transpose(0, 2, 1, 3).reshape(2, 1, TILE, TILE, QD)


def solution(mesh):
    in_specs = (P("tm", "ha", None, None, None), P(), P(), P(), P("tm"), P())
    out_specs = P("tm", "ha", None, None, None)
    return jax.shard_map(shards, mesh=mesh, in_specs=in_specs, out_specs=out_specs, check_vma=False)
```

```python
import functools
import math

import jax
import jax.numpy as jnp
from jax import lax
from jax.experimental import pallas as pl
from jax.experimental.pallas import tpu as pltpu
from jax.sharding import PartitionSpec as P

D = 1536
HEADS = 6
HD = 128
TILE = 16
PAD = 2
TOKENS = TILE * TILE
QD = HEADS * HD
FRAMES = 32
CHIPS = 16
SLOTS = 8
RIM = 112
LENGTH = 3 * TOKENS + 2 * RIM
LOWEST = -1e30
LOG2E = math.log2(math.e)
SCALE = LOG2E / math.sqrt(HD)
AXES = ("tm", "ha")


def project_kernel(info, tokens_hbm, weights, gains, modulation, own, away, inputs, tokens, rows, sem):
    part = pl.program_id(0)
    core = info[0]

    @pl.when(part == 0)
    def _():
        copies = [pltpu.make_async_copy(tokens_hbm, tokens, sem.at[0])]
        for frame in range(2):
            copies.append(pltpu.make_async_copy(modulation.at[info[1 + frame]], rows.at[frame], sem.at[1 + frame]))
        for copy in copies:
            copy.start()
        for copy in copies:
            copy.wait()
        for turn in range(2):
            frame = 1 - core if turn == 0 else core
            values = tokens[frame].astype(jnp.float32)
            average = jnp.mean(values, axis=-1, keepdims=True)
            centred = values - average
            spread = jnp.mean(centred * centred, axis=-1, keepdims=True)
            normed = centred * lax.rsqrt(spread + 1e-06)
            shift = rows[frame, 0:1, :]
            scale = rows[frame, 1:2, :]
            inputs[pl.ds(turn * TOKENS, TOKENS)] = (normed * (1.0 + scale) + shift).astype(jnp.bfloat16)

    raw = jnp.dot(inputs[...], weights[...], preferred_element_type=jnp.float32)

    def put(result):
        result = result.astype(jnp.bfloat16)
        for head in range(HEADS):
            columns = slice(head * HD, (head + 1) * HD)
            away[head] = result[:TOKENS, columns]
            own[head] = result[TOKENS:, columns]

    @pl.when(part < 2)
    def _():
        row = jnp.where(part == 0, gains[0:1, :], gains[1:2, :])
        put(raw * lax.rsqrt(jnp.mean(raw * raw, axis=-1, keepdims=True) + 1e-06) * row)

    @pl.when(part == 2)
    def _():
        put(raw)


def in_hbm(value):
    return pltpu.with_memory_space_constraint(value, pltpu.HBM)


def project(tokens, projection, norm_gain, modulation, levels, core):
    info = jnp.concatenate([core[None], levels])
    return pl.pallas_call(
        project_kernel,
        grid_spec=pltpu.PrefetchScalarGridSpec(
            num_scalar_prefetch=1,
            grid=(3,),
            in_specs=[
                pl.BlockSpec(memory_space=pltpu.HBM),
                pl.BlockSpec((D, QD), lambda p, info: (0, p)),
                pl.BlockSpec((2, QD), lambda p, info: (0, 0)),
                pl.BlockSpec(memory_space=pltpu.HBM),
            ],
            out_specs=[
                pl.BlockSpec((SLOTS, TOKENS, HD), lambda p, info: (info[0], p, 0)),
                pl.BlockSpec((SLOTS, TOKENS, HD), lambda p, info: (0, p, 0)),
            ],
            scratch_shapes=[
                pltpu.VMEM((2 * TOKENS, D), jnp.bfloat16),
                pltpu.VMEM((2, TOKENS, D), jnp.bfloat16),
                pltpu.VMEM((2, 2, D), jnp.float32),
                pltpu.SemaphoreType.DMA((3,)),
            ],
        ),
        out_shape=[
            jax.ShapeDtypeStruct((CHIPS, LENGTH, HD), jnp.bfloat16),
            jax.ShapeDtypeStruct((SLOTS, 3 * TOKENS, HD), jnp.bfloat16),
        ],
        compiler_params=pltpu.CompilerParams(vmem_limit_bytes=48 * 1024 * 1024),
        name="project",
    )(info, in_hbm(tokens), projection, norm_gain, in_hbm(modulation))


STREAMS = 4
EACH = CHIPS // STREAMS
WIDE = 512
PIECE = 256
LIMIT = EACH * (FRAMES * TOKENS // WIDE)
ROWS = STREAMS * (EACH + 1)


def plan(core, size, slots, bits, chips, pick, block, left):
    def visit(turn, carry):
        place = carry[0]
        time = FRAMES - 1 - turn
        slot = slots[time]
        mine = (slot + bits[slot // 2] + core) % 2 == 0
        lane = place % (2 * STREAMS)
        stream = jnp.where(lane < STREAMS, lane, 2 * STREAMS - 1 - lane)
        row = place // STREAMS
        rows = (time + 1) * size
        count = jnp.where(mine, (rows + WIDE - 1) // WIDE, 0)
        used = carry[1]
        for other in range(1, STREAMS):
            used = jnp.where(stream == other, carry[1 + other], used)

        @pl.when(mine)
        def _():
            chips[row * STREAMS + stream] = slot // 2

        def fill(step, inner):
            pick[stream, used + step] = row
            block[stream, used + step] = step
            left[stream, used + step] = rows - step * WIDE
            return inner

        lax.fori_loop(0, count, fill, 0)
        grown = tuple(carry[1 + s] + jnp.where(stream == s, count, 0) for s in range(STREAMS))
        return (place + jnp.where(mine, 1, 0),) + grown

    zero = jnp.int32(0)
    totals = lax.fori_loop(0, FRAMES, visit, (zero,) + (zero,) * STREAMS)[1:]
    trip = functools.reduce(jnp.maximum, totals)
    for stream in range(STREAMS):

        def clear(step, carry):
            pick[stream, step] = EACH
            block[stream, step] = 0
            left[stream, step] = WIDE
            return carry

        lax.fori_loop(totals[stream], trip + 2, clear, 0)
    return trip


def fold(values, combine):
    return combine(values.reshape(values.shape[0] // 8, 8, values.shape[1]), axis=0)


def sweep(trip, scored, queries, keys, values, tops, totals, mixes, pick, block, left, raws, peaks):
    def spots_of(step):
        spots = []
        for stream in range(STREAMS):
            row = pick[stream, step] * STREAMS + stream
            first = pl.multiple_of(block[stream, step] * WIDE, WIDE)
            spots.append((row, first, left[stream, step]))
        return spots

    def ask(spot, part):
        row, first, remain = spot
        rows = pl.ds(pl.multiple_of(first + part * PIECE, PIECE), PIECE)
        raw = jnp.dot(keys[rows], queries[row], preferred_element_type=jnp.float32)
        return scored(raw, rows, remain - part * PIECE)

    def advance(step, slot):
        now = spots_of(step)
        then = spots_of(step + 1)
        state = []
        for stream, (row, first, remain) in enumerate(now):
            highest = jnp.max(peaks[slot][stream][...], axis=0, keepdims=True) * SCALE
            top = tops[row]
            newest = jnp.maximum(top, highest)
            rescale = jnp.exp2(top - newest)
            state.append([newest, totals[row] * rescale, mixes[row] * rescale[0:1], None])
        for part in range(WIDE // PIECE):
            span = slice(part * PIECE, (part + 1) * PIECE)
            for stream, (row, first, remain) in enumerate(now):
                raw = ask(then[stream], part)
                raws[1 - slot][stream][span] = raw
                peak = fold(raw, jnp.max)
                held = state[stream]
                held[3] = peak if part == 0 else jnp.maximum(held[3], peak)
                weights = jnp.exp2(raws[slot][stream][span] * SCALE - held[0][0:1])
                held[1] = held[1] + fold(weights, jnp.sum)
                columns = pl.ds(pl.multiple_of(first + part * PIECE, PIECE), PIECE)
                held[2] = held[2] + jnp.dot(values[:, columns], weights.astype(jnp.bfloat16), preferred_element_type=jnp.float32)
        for stream, (row, first, remain) in enumerate(now):
            tops[row], totals[row], mixes[row], peaks[1 - slot][stream][...] = state[stream]

    def body(pair, carry):
        advance(2 * pair, 0)
        advance(2 * pair + 1, 1)
        return carry

    for stream, spot in enumerate(spots_of(0)):
        for part in range(WIDE // PIECE):
            raw = ask(spot, part)
            raws[0][stream][part * PIECE : (part + 1) * PIECE] = raw
            peak = fold(raw, jnp.max)
            peaks[0][stream][...] = peak if part == 0 else jnp.maximum(peaks[0][stream][...], peak)
    lax.fori_loop(0, (trip + 1) // 2, body, 0)


def gather_frames(slots, core, near, far, moves, sem):
    def start(time, carry):
        slot = slots[time]
        chip = slot // 2
        mine = slot % 2 == core

        def copy(source):
            for number, (first, size, target) in enumerate(moves):
                rows = pl.ds(pl.multiple_of(time * size, size), size)
                pltpu.make_async_copy(source.at[chip, pl.ds(first, size)], target.at[rows], sem.at[number]).start()

        pl.when(mine)(lambda: copy(near))
        pl.when(jnp.logical_not(mine))(lambda: copy(far))
        return carry

    lax.fori_loop(0, FRAMES, start, 0)


def turn_values(staged, values, total):
    def turn(step, carry):
        rows = pl.ds(pl.multiple_of(step * WIDE, WIDE), WIDE)
        values[:, rows] = staged[rows].T
        return carry

    lax.fori_loop(0, total // WIDE, turn, 0)


def turn_queries(chips, staged, queries):
    for place in range(CHIPS):
        queries[place] = staged[chips[place]].T


def attend_kernel(info, near, far, bias, out, bits, *scratch):
    tops, totals, mixes, asked, queries, keys, staged, values, rim_keys, rim_staged, rim_values, slots, chips = scratch[:13]
    lists, rim_lists, sem, raws = scratch[13:16], scratch[16:19], scratch[19], scratch[20:]
    raws, peaks = raws[: 2 * STREAMS], raws[2 * STREAMS :]
    raws, peaks = [(r[:STREAMS], r[STREAMS:]) for r in (raws, peaks)]
    core = info[FRAMES]
    for slot in range(FRAMES):
        slots[info[slot]] = slot
    ahead = jnp.int32(0)
    for chip in range(CHIPS):
        even = info[2 * chip]
        odd = info[2 * chip + 1]
        turned = (ahead >= 0) == (even > odd)
        bits[chip] = jnp.where(turned, 1, 0)
        ahead = ahead + jnp.where(turned, odd - even, even - odd)

        def ask(source):
            pltpu.make_async_copy(source.at[chip, pl.ds(0, TOKENS)], asked.at[chip], sem.at[4]).start()

        pl.when(turned)(lambda: ask(far))
        pl.when(jnp.logical_not(turned))(lambda: ask(near))
    rim_at = 3 * TOKENS
    moves = (
        (TOKENS, TOKENS, keys),
        (2 * TOKENS, TOKENS, staged),
        (rim_at, RIM, rim_keys),
        (rim_at + RIM, RIM, rim_staged),
    )
    gather_frames(slots, core, near, far, moves, sem)
    trip = plan(core, TOKENS, slots, bits, chips, *lists)
    rim_trip = plan(core, RIM, slots, bits, chips, *rim_lists)
    tops[...] = jnp.full(tops.shape, LOWEST, jnp.float32)
    totals[...] = jnp.zeros(totals.shape, jnp.float32)
    mixes[...] = jnp.zeros(mixes.shape, jnp.float32)
    queries[pl.ds(CHIPS, STREAMS)] = jnp.zeros((STREAMS, HD, TOKENS), jnp.bfloat16)
    pltpu.make_async_copy(asked, asked, sem.at[4]).wait()
    turn_queries(chips, asked, queries)
    for number, move in enumerate(moves):
        pltpu.make_async_copy(move[2], move[2], sem.at[number]).wait()
    turn_values(staged, values, FRAMES * TOKENS)
    turn_values(rim_staged, rim_values, FRAMES * RIM)

    def scored(raw, rows, remain):
        return raw + jnp.where(remain <= 0, LOWEST, 0.0)

    sweep(trip, scored, queries, keys, values, tops, totals, mixes, *lists, raws, peaks)

    def rim_scored(raw, rows, remain):
        place = lax.broadcasted_iota(jnp.int32, (PIECE, HD), 0)
        added = jnp.where(place < remain, bias[rows], LOWEST)
        return jnp.concatenate([raw[:, :HD] + added, raw[:, HD:] + added], axis=1)

    sweep(rim_trip, rim_scored, queries, rim_keys, rim_values, tops, totals, mixes, *rim_lists, raws, peaks)
    for place in range(CHIPS):
        whole = jnp.sum(totals[place], axis=0, keepdims=True)
        out[chips[place]] = (mixes[place] / whole).T.astype(jnp.bfloat16)


def attend(info, near, far, bias):
    lists = [pltpu.SMEM((STREAMS, LIMIT + 2), jnp.int32)] * 3
    return pl.pallas_call(
        attend_kernel,
        grid_spec=pltpu.PrefetchScalarGridSpec(
            num_scalar_prefetch=1,
            grid=(1,),
            in_specs=[
                pl.BlockSpec(memory_space=pl.ANY),
                pl.BlockSpec(memory_space=pl.ANY),
                pl.BlockSpec(bias.shape, lambda i, info: (0, 0)),
            ],
            out_specs=[
                pl.BlockSpec((CHIPS, TOKENS, HD), lambda i, info: (0, 0, 0)),
                pl.BlockSpec(memory_space=pltpu.SMEM),
            ],
            scratch_shapes=[
                pltpu.VMEM((ROWS, 8, TOKENS), jnp.float32),
                pltpu.VMEM((ROWS, 8, TOKENS), jnp.float32),
                pltpu.VMEM((ROWS, HD, TOKENS), jnp.float32),
                pltpu.VMEM((CHIPS, TOKENS, HD), jnp.bfloat16),
                pltpu.VMEM((ROWS, HD, TOKENS), jnp.bfloat16),
                pltpu.VMEM((FRAMES * TOKENS, HD), jnp.bfloat16),
                pltpu.VMEM((FRAMES * TOKENS, HD), jnp.bfloat16),
                pltpu.VMEM((HD, FRAMES * TOKENS), jnp.bfloat16),
                pltpu.VMEM((FRAMES * RIM, HD), jnp.bfloat16),
                pltpu.VMEM((FRAMES * RIM, HD), jnp.bfloat16),
                pltpu.VMEM((HD, FRAMES * RIM), jnp.bfloat16),
                pltpu.SMEM((FRAMES,), jnp.int32),
                pltpu.SMEM((CHIPS,), jnp.int32),
            ]
            + lists
            + lists
            + [pltpu.SemaphoreType.DMA((5,))]
            + [pltpu.VMEM((WIDE, TOKENS), jnp.float32)] * (2 * STREAMS)
            + [pltpu.VMEM((8, TOKENS), jnp.float32)] * (2 * STREAMS),
        ),
        out_shape=[
            jax.ShapeDtypeStruct((CHIPS, TOKENS, HD), jnp.bfloat16),
            jax.ShapeDtypeStruct((CHIPS,), jnp.int32),
        ],
        compiler_params=pltpu.CompilerParams(vmem_limit_bytes=48 * 1024 * 1024),
        name="attend",
    )(info, near, far, bias)


def swap_cores(value):
    return lax.ppermute(value, "ha", [(i, i ^ 1) for i in range(8)])


def swap_depth(value, bits):
    return lax.ppermute(value, "ha", [(i, i ^ (2 * bits)) for i in range(8)])


def rim_rows(pair, depth):
    even = depth % 2 == 0
    upper = depth < 2

    def edge(strip):
        return jnp.where(upper, strip[..., TILE - PAD :, :, :], strip[..., :PAD, :, :])

    sent = jnp.where(even, pair[1, :, :, :, TILE - PAD :], pair[0, :, :, :, :PAD])
    outer = swap_depth(sent, 1)
    above = swap_depth(edge(pair), 2)
    corner = swap_depth(edge(sent), 3)
    inner = (pair[1, :, :, :, :PAD], pair[0, :, :, :, TILE - PAD :])
    inner_corner = (above[1, :, :, :, :PAD], above[0, :, :, :, TILE - PAD :])
    spare = jnp.zeros((SLOTS, 2, RIM - 104, HD), jnp.bfloat16)

    def flat(piece):
        return piece.reshape(SLOTS, 2, -1, HD)

    both = []
    for tile in range(2):
        rows = [inner[tile], above[tile], inner_corner[tile], outer, corner]
        both.append(jnp.concatenate([flat(r) for r in rows] + [spare], axis=2))
    return jnp.concatenate(both, axis=0).reshape(CHIPS, 2 * RIM, HD)


def rim_bias(outer_valid):
    place = jnp.arange(RIM, dtype=jnp.int32)
    valid = (place < 68) | ((place < 104) & outer_valid)
    column_of = jnp.tile(jnp.where(valid, 0.0, LOWEST).astype(jnp.float32), FRAMES)
    return jnp.broadcast_to(column_of[:, None], (FRAMES * RIM, HD))


def shards(tokens, projection, norm_gain, modulation, levels, frame_order):
    chip = lax.axis_index("tm")
    place = lax.axis_index("ha")
    depth = place // 2
    core = place % 2
    sending, away = project(tokens.reshape(2, TOKENS, D), projection, norm_gain, modulation, levels, core)
    other = swap_cores(away)
    first = (1 - core) * SLOTS
    sending = lax.dynamic_update_slice(sending, other, (first, 0, 0))
    pair = sending[:, TOKENS : 3 * TOKENS].reshape(2, SLOTS, 2, TILE, TILE, HD)
    sending = lax.dynamic_update_slice(sending, rim_rows(pair, depth), (0, 3 * TOKENS, 0))
    received = lax.all_to_all(sending, "tm", 0, 0, tiled=True)
    far = swap_cores(received)

    info = jnp.concatenate([frame_order, core[None]])
    odd_tile = chip // SLOTS
    bias = rim_bias(depth % 2 != odd_tile)
    mixed, bits = attend(info, received, far, bias)
    turned = lax.dynamic_index_in_dim(bits, chip, 0, keepdims=False)

    back = lax.all_to_all(mixed, "tm", 0, 0, tiled=True)
    stay = lax.dynamic_slice_in_dim(back, core * SLOTS, HEADS, 0)
    leave = lax.dynamic_slice_in_dim(back, (1 - core) * SLOTS, HEADS, 0)
    come = swap_cores(leave)
    both = jnp.where(core == turned, jnp.stack([stay, come]), jnp.stack([come, stay]))
    return both.transpose(0, 2, 1, 3).reshape(2, 1, TILE, TILE, QD)


def solution(mesh):
    in_specs = (P("tm", "ha", None, None, None), P(), P(), P(), P("tm"), P())
    out_specs = P("tm", "ha", None, None, None)
    return jax.shard_map(shards, mesh=mesh, in_specs=in_specs, out_specs=out_specs, check_vma=False)
```

```python
import functools
import math

import jax
import jax.numpy as jnp
from jax import lax
from jax.experimental import pallas as pl
from jax.experimental.pallas import tpu as pltpu
from jax.sharding import PartitionSpec as P

D = 1536
HEADS = 6
HD = 128
TILE = 16
PAD = 2
TOKENS = TILE * TILE
QD = HEADS * HD
FRAMES = 32
CHIPS = 16
SLOTS = 8
RIM = 112
LENGTH = 3 * TOKENS + 2 * RIM
LOWEST = -1e30
LOG2E = math.log2(math.e)
SCALE = LOG2E / math.sqrt(HD)
AXES = ("tm", "ha")


def project_kernel(info, tokens_hbm, weights, gains, modulation, own, away, inputs, tokens, rows, sem):
    part = pl.program_id(0)
    core = info[0]

    @pl.when(part == 0)
    def _():
        copies = [pltpu.make_async_copy(tokens_hbm, tokens, sem.at[0])]
        for frame in range(2):
            copies.append(pltpu.make_async_copy(modulation.at[info[1 + frame]], rows.at[frame], sem.at[1 + frame]))
        for copy in copies:
            copy.start()
        for copy in copies:
            copy.wait()
        for turn in range(2):
            frame = 1 - core if turn == 0 else core
            values = tokens[frame].astype(jnp.float32)
            average = jnp.mean(values, axis=-1, keepdims=True)
            centred = values - average
            spread = jnp.mean(centred * centred, axis=-1, keepdims=True)
            normed = centred * lax.rsqrt(spread + 1e-06)
            shift = rows[frame, 0:1, :]
            scale = rows[frame, 1:2, :]
            inputs[pl.ds(turn * TOKENS, TOKENS)] = (normed * (1.0 + scale) + shift).astype(jnp.bfloat16)

    raw = jnp.dot(inputs[...], weights[...], preferred_element_type=jnp.float32)

    def put(result):
        result = result.astype(jnp.bfloat16)
        for head in range(HEADS):
            columns = slice(head * HD, (head + 1) * HD)
            away[head] = result[:TOKENS, columns]
            own[head] = result[TOKENS:, columns]

    @pl.when(part < 2)
    def _():
        row = jnp.where(part == 0, gains[0:1, :], gains[1:2, :])
        put(raw * lax.rsqrt(jnp.mean(raw * raw, axis=-1, keepdims=True) + 1e-06) * row)

    @pl.when(part == 2)
    def _():
        put(raw)


def in_hbm(value):
    return pltpu.with_memory_space_constraint(value, pltpu.HBM)


def project(tokens, projection, norm_gain, modulation, levels, core):
    info = jnp.concatenate([core[None], levels])
    return pl.pallas_call(
        project_kernel,
        grid_spec=pltpu.PrefetchScalarGridSpec(
            num_scalar_prefetch=1,
            grid=(3,),
            in_specs=[
                pl.BlockSpec(memory_space=pltpu.HBM),
                pl.BlockSpec((D, QD), lambda p, info: (0, p)),
                pl.BlockSpec((2, QD), lambda p, info: (0, 0)),
                pl.BlockSpec(memory_space=pltpu.HBM),
            ],
            out_specs=[
                pl.BlockSpec((SLOTS, TOKENS, HD), lambda p, info: (info[0], p, 0)),
                pl.BlockSpec((HEADS, TOKENS, HD), lambda p, info: (0, p, 0)),
            ],
            scratch_shapes=[
                pltpu.VMEM((2 * TOKENS, D), jnp.bfloat16),
                pltpu.VMEM((2, TOKENS, D), jnp.bfloat16),
                pltpu.VMEM((2, 2, D), jnp.float32),
                pltpu.SemaphoreType.DMA((3,)),
            ],
        ),
        out_shape=[
            jax.ShapeDtypeStruct((CHIPS, LENGTH, HD), jnp.bfloat16),
            jax.ShapeDtypeStruct((HEADS, 3 * TOKENS, HD), jnp.bfloat16),
        ],
        compiler_params=pltpu.CompilerParams(vmem_limit_bytes=48 * 1024 * 1024),
        name="project",
    )(info, in_hbm(tokens), projection, in_hbm(norm_gain), in_hbm(modulation))


STREAMS = 4
EACH = CHIPS // STREAMS
WIDE = 512
PIECE = 256
LIMIT = EACH * (FRAMES * TOKENS // WIDE)
ROWS = STREAMS * (EACH + 1)


def plan(core, slots, bits, chips, seen, items, rim_items):
    sizes = ((TOKENS, items), (RIM, rim_items))

    def visit(turn, carry):
        place = carry[0]
        time = FRAMES - 1 - turn
        slot = slots[time]
        mine = (slot + bits[slot // 2] + core) % 2 == 0
        lane = place % (2 * STREAMS)
        stream = jnp.where(lane < STREAMS, lane, 2 * STREAMS - 1 - lane)
        row = place // STREAMS

        @pl.when(mine)
        def _():
            chips[row * STREAMS + stream] = slot // 2
            seen[row * STREAMS + stream] = time + 1
            for number, (size, target) in enumerate(sizes):
                count = ((time + 1) * size + WIDE - 1) // WIDE
                used = chips[CHIPS + number * STREAMS + stream]

                def fill(step, inner):
                    target[stream, used + step] = row * WIDE + step
                    return inner

                lax.fori_loop(0, count, fill, 0)
                chips[CHIPS + number * STREAMS + stream] = used + count

        return (place + jnp.where(mine, 1, 0),)

    for number in range(2 * STREAMS):
        chips[CHIPS + number] = 0
    for stream in range(STREAMS):
        seen[CHIPS + stream] = FRAMES
    lax.fori_loop(0, FRAMES, visit, (jnp.int32(0),))
    trips = []
    for number, (size, target) in enumerate(sizes):
        totals = [chips[CHIPS + number * STREAMS + stream] for stream in range(STREAMS)]
        trip = functools.reduce(jnp.maximum, totals)
        for stream in range(STREAMS):

            def clear(step, carry):
                target[stream, step] = EACH * WIDE
                return carry

            lax.fori_loop(totals[stream], trip + 2, clear, 0)
        trips.append(trip)
    return trips


def fold(values, combine):
    return combine(values.reshape(values.shape[0] // 8, 8, values.shape[1]), axis=0)


def sweep(trip, scored, queries, keys, values, tops, totals, mixes, items, seen, size, raws, peaks):
    def spots_of(step):
        spots = []
        for stream in range(STREAMS):
            item = items[stream, step]
            row = item // WIDE * STREAMS + stream
            first = pl.multiple_of(item % WIDE * WIDE, WIDE)
            spots.append((row, first, seen[row] * size - first))
        return spots

    def ask(spot, part):
        row, first, remain = spot
        rows = pl.ds(pl.multiple_of(first + part * PIECE, PIECE), PIECE)
        raw = jnp.dot(keys[rows], queries[row], preferred_element_type=jnp.float32)
        return scored(raw, rows, remain - part * PIECE)

    def advance(step, slot):
        now = spots_of(step)
        then = spots_of(step + 1)
        state = []
        for stream, (row, first, remain) in enumerate(now):
            highest = jnp.max(peaks[slot][stream][...], axis=0, keepdims=True) * SCALE
            top = tops[row]
            newest = jnp.maximum(top, highest)
            rescale = jnp.exp2(top - newest)
            state.append([newest, totals[row] * rescale, mixes[row] * rescale[0:1], None])
        for part in range(WIDE // PIECE):
            span = slice(part * PIECE, (part + 1) * PIECE)
            for stream, (row, first, remain) in enumerate(now):
                raw = ask(then[stream], part)
                raws[1 - slot][stream][span] = raw
                peak = fold(raw, jnp.max)
                held = state[stream]
                held[3] = peak if part == 0 else jnp.maximum(held[3], peak)
                weights = jnp.exp2(raws[slot][stream][span] * SCALE - held[0][0:1])
                held[1] = held[1] + fold(weights, jnp.sum)
                columns = pl.ds(pl.multiple_of(first + part * PIECE, PIECE), PIECE)
                held[2] = held[2] + jnp.dot(values[:, columns], weights.astype(jnp.bfloat16), preferred_element_type=jnp.float32)
        for stream, (row, first, remain) in enumerate(now):
            tops[row], totals[row], mixes[row], peaks[1 - slot][stream][...] = state[stream]

    def body(pair, carry):
        advance(2 * pair, 0)
        advance(2 * pair + 1, 1)
        return carry

    for stream, spot in enumerate(spots_of(0)):
        for part in range(WIDE // PIECE):
            raw = ask(spot, part)
            raws[0][stream][part * PIECE : (part + 1) * PIECE] = raw
            peak = fold(raw, jnp.max)
            peaks[0][stream][...] = peak if part == 0 else jnp.maximum(peaks[0][stream][...], peak)
    lax.fori_loop(0, (trip + 1) // 2, body, 0)


def gather_frames(slots, core, near, far, moves, sem):
    def start(time, carry):
        slot = slots[time]
        chip = slot // 2
        mine = slot % 2 == core

        def copy(source):
            for number, (first, size, target) in enumerate(moves):
                rows = pl.ds(pl.multiple_of(time * size, size), size)
                pltpu.make_async_copy(source.at[chip, pl.ds(first, size)], target.at[rows], sem.at[number]).start()

        pl.when(mine)(lambda: copy(near))
        pl.when(jnp.logical_not(mine))(lambda: copy(far))
        return carry

    lax.fori_loop(0, FRAMES, start, 0)


def turn_values(staged, values, total):
    def turn(step, carry):
        rows = pl.ds(pl.multiple_of(step * WIDE, WIDE), WIDE)
        values[:, rows] = staged[rows].T
        return carry

    lax.fori_loop(0, total // WIDE, turn, 0)


def turn_queries(chips, staged, queries):
    for place in range(CHIPS):
        queries[place] = staged[chips[place]].T


def attend_kernel(info, near, far, bias, out, bits, *scratch):
    tops, totals, mixes, asked, queries, keys, staged, values, rim_keys, rim_staged, rim_values, slots, chips = scratch[:13]
    seen, items, rim_items, sem = scratch[13:17]
    raws = scratch[17:]
    raws, peaks = raws[: 2 * STREAMS], raws[2 * STREAMS :]
    raws, peaks = [(r[:STREAMS], r[STREAMS:]) for r in (raws, peaks)]
    core = info[FRAMES]
    for slot in range(FRAMES):
        slots[info[slot]] = slot
    ahead = jnp.int32(0)
    for chip in range(CHIPS):
        even = info[2 * chip]
        odd = info[2 * chip + 1]
        turned = (ahead >= 0) == (even > odd)
        bits[chip] = jnp.where(turned, 1, 0)
        ahead = ahead + jnp.where(turned, odd - even, even - odd)

        def ask(source):
            pltpu.make_async_copy(source.at[chip, pl.ds(0, TOKENS)], asked.at[chip], sem.at[4]).start()

        pl.when(turned)(lambda: ask(far))
        pl.when(jnp.logical_not(turned))(lambda: ask(near))
    rim_at = 3 * TOKENS
    moves = (
        (TOKENS, TOKENS, keys),
        (2 * TOKENS, TOKENS, staged),
        (rim_at, RIM, rim_keys),
        (rim_at + RIM, RIM, rim_staged),
    )
    gather_frames(slots, core, near, far, moves, sem)
    trip, rim_trip = plan(core, slots, bits, chips, seen, items, rim_items)
    tops[...] = jnp.full(tops.shape, LOWEST, jnp.float32)
    totals[...] = jnp.zeros(totals.shape, jnp.float32)
    mixes[...] = jnp.zeros(mixes.shape, jnp.float32)
    queries[pl.ds(CHIPS, STREAMS)] = jnp.zeros((STREAMS, HD, TOKENS), jnp.bfloat16)
    pltpu.make_async_copy(asked, asked, sem.at[4]).wait()
    turn_queries(chips, asked, queries)
    for number, move in enumerate(moves):
        pltpu.make_async_copy(move[2], move[2], sem.at[number]).wait()
    turn_values(staged, values, FRAMES * TOKENS)
    turn_values(rim_staged, rim_values, FRAMES * RIM)

    def scored(raw, rows, remain):
        return raw + jnp.where(remain <= 0, LOWEST, 0.0)

    sweep(trip, scored, queries, keys, values, tops, totals, mixes, items, seen, TOKENS, raws, peaks)

    def rim_scored(raw, rows, remain):
        place = lax.broadcasted_iota(jnp.int32, (PIECE, HD), 0)
        added = jnp.where(place < remain, bias[rows], LOWEST)
        return jnp.concatenate([raw[:, :HD] + added, raw[:, HD:] + added], axis=1)

    sweep(rim_trip, rim_scored, queries, rim_keys, rim_values, tops, totals, mixes, rim_items, seen, RIM, raws, peaks)
    for place in range(CHIPS):
        whole = jnp.sum(totals[place], axis=0, keepdims=True)
        out[chips[place]] = (mixes[place] / whole).T.astype(jnp.bfloat16)


def attend(info, near, far, bias):
    return pl.pallas_call(
        attend_kernel,
        grid_spec=pltpu.PrefetchScalarGridSpec(
            num_scalar_prefetch=1,
            grid=(1,),
            in_specs=[
                pl.BlockSpec(memory_space=pl.ANY),
                pl.BlockSpec(memory_space=pl.ANY),
                pl.BlockSpec(bias.shape, lambda i, info: (0, 0)),
            ],
            out_specs=[
                pl.BlockSpec((CHIPS, TOKENS, HD), lambda i, info: (0, 0, 0)),
                pl.BlockSpec(memory_space=pltpu.SMEM),
            ],
            scratch_shapes=[
                pltpu.VMEM((ROWS, 8, TOKENS), jnp.float32),
                pltpu.VMEM((ROWS, 8, TOKENS), jnp.float32),
                pltpu.VMEM((ROWS, HD, TOKENS), jnp.float32),
                pltpu.VMEM((CHIPS, TOKENS, HD), jnp.bfloat16),
                pltpu.VMEM((ROWS, HD, TOKENS), jnp.bfloat16),
                pltpu.VMEM((FRAMES * TOKENS, HD), jnp.bfloat16),
                pltpu.VMEM((FRAMES * TOKENS, HD), jnp.bfloat16),
                pltpu.VMEM((HD, FRAMES * TOKENS), jnp.bfloat16),
                pltpu.VMEM((FRAMES * RIM, HD), jnp.bfloat16),
                pltpu.VMEM((FRAMES * RIM, HD), jnp.bfloat16),
                pltpu.VMEM((HD, FRAMES * RIM), jnp.bfloat16),
                pltpu.SMEM((FRAMES,), jnp.int32),
                pltpu.SMEM((CHIPS + 2 * STREAMS,), jnp.int32),
                pltpu.SMEM((ROWS,), jnp.int32),
                pltpu.SMEM((STREAMS, LIMIT + 2), jnp.int32),
                pltpu.SMEM((STREAMS, LIMIT + 2), jnp.int32),
            ]
            + [pltpu.SemaphoreType.DMA((5,))]
            + [pltpu.VMEM((WIDE, TOKENS), jnp.float32)] * (2 * STREAMS)
            + [pltpu.VMEM((8, TOKENS), jnp.float32)] * (2 * STREAMS),
        ),
        out_shape=[
            jax.ShapeDtypeStruct((CHIPS, TOKENS, HD), jnp.bfloat16),
            jax.ShapeDtypeStruct((CHIPS,), jnp.int32),
        ],
        compiler_params=pltpu.CompilerParams(vmem_limit_bytes=48 * 1024 * 1024),
        name="attend",
    )(info, near, far, bias)


def swap_cores(value):
    return lax.ppermute(value, "ha", [(i, i ^ 1) for i in range(8)])


def swap_depth(value, bits):
    return lax.ppermute(value, "ha", [(i, i ^ (2 * bits)) for i in range(8)])


def rim_rows(sending, depth):
    lines = sending.reshape(2, SLOTS, LENGTH // TILE, TILE, HD)
    even = depth % 2 == 0
    upper = depth < 2

    def strip(tile, first):
        piece = lines[tile, :HEADS, TILE : 3 * TILE, first : first + PAD]
        return piece.reshape(HEADS, 2, TILE, PAD, HD)

    def bottom_or_top(value, axis):
        low = lax.slice_in_dim(value, TILE - PAD, TILE, axis=axis)
        return jnp.where(upper, low, lax.slice_in_dim(value, 0, PAD, axis=axis))

    def edge(first):
        low = lines[:, :HEADS, first + TILE - PAD : first + TILE]
        return jnp.where(upper, low, lines[:, :HEADS, first : first + PAD])

    sent = jnp.where(even, strip(1, TILE - PAD), strip(0, 0))
    outer = swap_depth(sent, 1)
    above = swap_depth(jnp.stack([edge(TILE), edge(2 * TILE)], axis=2), 2)
    corner = swap_depth(bottom_or_top(sent, 2), 3)
    inner = (strip(1, 0), strip(0, TILE - PAD))
    inner_corner = (above[1, :, :, :, :PAD], above[0, :, :, :, TILE - PAD :])
    spare = jnp.zeros((HEADS, 2, RIM - 104, HD), jnp.bfloat16)

    def flat(piece):
        return piece.reshape(HEADS, 2, -1, HD)

    both = []
    for tile in range(2):
        rows = [inner[tile], above[tile], inner_corner[tile], outer, corner]
        both.append(jnp.concatenate([flat(r) for r in rows] + [spare], axis=2))
    return jnp.stack(both).reshape(2, HEADS, 2 * RIM, HD)


def rim_bias(outer_valid):
    place = jnp.arange(RIM, dtype=jnp.int32)
    valid = (place < 68) | ((place < 104) & outer_valid)
    column_of = jnp.tile(jnp.where(valid, 0.0, LOWEST).astype(jnp.float32), FRAMES)
    return jnp.broadcast_to(column_of[:, None], (FRAMES * RIM, HD))


def shards(tokens, projection, norm_gain, modulation, levels, frame_order):
    chip = lax.axis_index("tm")
    place = lax.axis_index("ha")
    depth = place // 2
    core = place % 2
    sending, away = project(tokens.reshape(2, TOKENS, D), projection, norm_gain, modulation, levels, core)
    other = swap_cores(away)
    first = (1 - core) * SLOTS
    sending = lax.dynamic_update_slice(sending, other, (first, 0, 0))
    halves = sending.reshape(2, SLOTS, LENGTH, HD)
    halves = lax.dynamic_update_slice(halves, rim_rows(sending, depth), (0, 0, 3 * TOKENS, 0))
    sending = halves.reshape(CHIPS, LENGTH, HD)
    received = lax.all_to_all(sending, "tm", 0, 0, tiled=True)
    far = swap_cores(received)

    info = jnp.concatenate([frame_order, core[None]])
    odd_tile = chip // SLOTS
    bias = rim_bias(depth % 2 != odd_tile)
    mixed, bits = attend(info, received, far, bias)
    turned = lax.dynamic_index_in_dim(bits, chip, 0, keepdims=False)

    back = lax.all_to_all(mixed, "tm", 0, 0, tiled=True)
    stay = lax.dynamic_slice_in_dim(back, core * SLOTS, HEADS, 0)
    leave = lax.dynamic_slice_in_dim(back, (1 - core) * SLOTS, HEADS, 0)
    come = swap_cores(leave)
    both = jnp.where(core == turned, jnp.stack([stay, come]), jnp.stack([come, stay]))
    return both.transpose(0, 2, 1, 3).reshape(2, 1, TILE, TILE, QD)


def solution(mesh):
    in_specs = (P("tm", "ha", None, None, None), P(), P(), P(), P("tm"), P())
    out_specs = P("tm", "ha", None, None, None)
    return jax.shard_map(shards, mesh=mesh, in_specs=in_specs, out_specs=out_specs, check_vma=False)
```

```python
import functools
import math

import jax
import jax.numpy as jnp
from jax import lax
from jax.experimental import pallas as pl
from jax.experimental.pallas import tpu as pltpu
from jax.sharding import PartitionSpec as P

D = 1536
HEADS = 6
HD = 128
TILE = 16
PAD = 2
TOKENS = TILE * TILE
QD = HEADS * HD
FRAMES = 32
CHIPS = 16
SLOTS = 8
RIM = 112
LENGTH = 3 * TOKENS + 2 * RIM
LOWEST = -1e30
LOG2E = math.log2(math.e)
SCALE = LOG2E / math.sqrt(HD)
AXES = ("tm", "ha")


def project_kernel(info, tokens_hbm, weights, gains, modulation, own, away, inputs, tokens, rows, sem):
    part = pl.program_id(0)
    core = info[0]

    @pl.when(part == 0)
    def _():
        copies = [pltpu.make_async_copy(tokens_hbm, tokens, sem.at[0])]
        for frame in range(2):
            copies.append(pltpu.make_async_copy(modulation.at[info[1 + frame]], rows.at[frame], sem.at[1 + frame]))
        for copy in copies:
            copy.start()
        for copy in copies:
            copy.wait()
        for turn in range(2):
            frame = 1 - core if turn == 0 else core
            values = tokens[frame].astype(jnp.float32)
            average = jnp.mean(values, axis=-1, keepdims=True)
            centred = values - average
            spread = jnp.mean(centred * centred, axis=-1, keepdims=True)
            normed = centred * lax.rsqrt(spread + 1e-06)
            shift = rows[frame, 0:1, :]
            scale = rows[frame, 1:2, :]
            inputs[pl.ds(turn * TOKENS, TOKENS)] = (normed * (1.0 + scale) + shift).astype(jnp.bfloat16)

    raw = jnp.dot(inputs[...], weights[...], preferred_element_type=jnp.float32)

    def put(result):
        result = result.astype(jnp.bfloat16)
        for head in range(HEADS):
            columns = slice(head * HD, (head + 1) * HD)
            away[head] = result[:TOKENS, columns]
            own[head] = result[TOKENS:, columns]

    @pl.when(part < 2)
    def _():
        row = jnp.where(part == 0, gains[0:1, :], gains[1:2, :])
        put(raw * lax.rsqrt(jnp.mean(raw * raw, axis=-1, keepdims=True) + 1e-06) * row)

    @pl.when(part == 2)
    def _():
        put(raw)


def in_hbm(value):
    return pltpu.with_memory_space_constraint(value, pltpu.HBM)


def project(tokens, projection, norm_gain, modulation, levels, core):
    info = jnp.concatenate([core[None], levels])
    return pl.pallas_call(
        project_kernel,
        grid_spec=pltpu.PrefetchScalarGridSpec(
            num_scalar_prefetch=1,
            grid=(3,),
            in_specs=[
                pl.BlockSpec(memory_space=pltpu.HBM),
                pl.BlockSpec((D, QD), lambda p, info: (0, p)),
                pl.BlockSpec((2, QD), lambda p, info: (0, 0)),
                pl.BlockSpec(memory_space=pltpu.HBM),
            ],
            out_specs=[
                pl.BlockSpec((SLOTS, TOKENS, HD), lambda p, info: (info[0], p, 0)),
                pl.BlockSpec((HEADS, TOKENS, HD), lambda p, info: (0, p, 0)),
            ],
            scratch_shapes=[
                pltpu.VMEM((2 * TOKENS, D), jnp.bfloat16),
                pltpu.VMEM((2, TOKENS, D), jnp.bfloat16),
                pltpu.VMEM((2, 2, D), jnp.float32),
                pltpu.SemaphoreType.DMA((3,)),
            ],
        ),
        out_shape=[
            jax.ShapeDtypeStruct((CHIPS, LENGTH, HD), jnp.bfloat16),
            jax.ShapeDtypeStruct((HEADS, 3 * TOKENS, HD), jnp.bfloat16),
        ],
        compiler_params=pltpu.CompilerParams(vmem_limit_bytes=60 * 1024 * 1024),
        name="project",
    )(info, in_hbm(tokens), projection, in_hbm(norm_gain), in_hbm(modulation))


STREAMS = 4
EACH = CHIPS // STREAMS
WIDE = 512
PIECE = 256
LIMIT = EACH * (FRAMES * TOKENS // WIDE)
ROWS = STREAMS * (EACH + 1)


def plan(core, slots, bits, chips, seen, items, rim_items):
    sizes = ((TOKENS, items), (RIM, rim_items))

    def visit(turn, carry):
        place = carry[0]
        time = FRAMES - 1 - turn
        slot = slots[time]
        mine = (slot + bits[slot // 2] + core) % 2 == 0
        lane = place % (2 * STREAMS)
        stream = jnp.where(lane < STREAMS, lane, 2 * STREAMS - 1 - lane)
        row = place // STREAMS

        @pl.when(mine)
        def _():
            chips[row * STREAMS + stream] = slot // 2
            seen[row * STREAMS + stream] = time + 1
            for number, (size, target) in enumerate(sizes):
                count = ((time + 1) * size + WIDE - 1) // WIDE
                used = chips[CHIPS + number * STREAMS + stream]

                def fill(step, inner):
                    target[stream, used + step] = row * WIDE + step
                    return inner

                lax.fori_loop(0, count, fill, 0)
                chips[CHIPS + number * STREAMS + stream] = used + count

        return (place + jnp.where(mine, 1, 0),)

    for number in range(2 * STREAMS):
        chips[CHIPS + number] = 0
    for stream in range(STREAMS):
        seen[CHIPS + stream] = FRAMES
    lax.fori_loop(0, FRAMES, visit, (jnp.int32(0),))
    trips = []
    for number, (size, target) in enumerate(sizes):
        totals = [chips[CHIPS + number * STREAMS + stream] for stream in range(STREAMS)]
        trip = functools.reduce(jnp.maximum, totals)
        for stream in range(STREAMS):

            def clear(step, carry):
                target[stream, step] = EACH * WIDE
                return carry

            lax.fori_loop(totals[stream], trip + 2, clear, 0)
        trips.append(trip)
    return trips


def fold(values, combine):
    return combine(values.reshape(values.shape[0] // 8, 8, values.shape[1]), axis=0)


def sweep(trip, scored, queries, keys, values, tops, totals, mixes, items, seen, size, raws, peaks):
    def spots_of(step):
        spots = []
        for stream in range(STREAMS):
            item = items[stream, step]
            row = item // WIDE * STREAMS + stream
            first = pl.multiple_of(item % WIDE * WIDE, WIDE)
            spots.append((row, first, seen[row] * size - first))
        return spots

    def ask(spot, part):
        row, first, remain = spot
        rows = pl.ds(pl.multiple_of(first + part * PIECE, PIECE), PIECE)
        raw = jnp.dot(keys[rows], queries[row], preferred_element_type=jnp.float32)
        return scored(raw, rows, remain - part * PIECE)

    def advance(step, slot):
        now = spots_of(step)
        then = spots_of(step + 1)
        state = []
        for stream, (row, first, remain) in enumerate(now):
            highest = jnp.max(peaks[slot][stream][...], axis=0, keepdims=True) * SCALE
            top = tops[row]
            newest = jnp.maximum(top, highest)
            rescale = jnp.exp2(top - newest)
            state.append([newest, totals[row] * rescale, mixes[row] * rescale[0:1], None])
        for part in range(WIDE // PIECE):
            span = slice(part * PIECE, (part + 1) * PIECE)
            for stream, (row, first, remain) in enumerate(now):
                raw = ask(then[stream], part)
                raws[1 - slot][stream][span] = raw
                peak = fold(raw, jnp.max)
                held = state[stream]
                held[3] = peak if part == 0 else jnp.maximum(held[3], peak)
                weights = jnp.exp2(raws[slot][stream][span] * SCALE - held[0][0:1])
                held[1] = held[1] + fold(weights, jnp.sum)
                columns = pl.ds(pl.multiple_of(first + part * PIECE, PIECE), PIECE)
                held[2] = held[2] + jnp.dot(values[:, columns], weights.astype(jnp.bfloat16), preferred_element_type=jnp.float32)
        for stream, (row, first, remain) in enumerate(now):
            tops[row], totals[row], mixes[row], peaks[1 - slot][stream][...] = state[stream]

    def body(pair, carry):
        advance(2 * pair, 0)
        advance(2 * pair + 1, 1)
        return carry

    for stream, spot in enumerate(spots_of(0)):
        for part in range(WIDE // PIECE):
            raw = ask(spot, part)
            raws[0][stream][part * PIECE : (part + 1) * PIECE] = raw
            peak = fold(raw, jnp.max)
            peaks[0][stream][...] = peak if part == 0 else jnp.maximum(peaks[0][stream][...], peak)
    lax.fori_loop(0, (trip + 1) // 2, body, 0)


def gather_frames(slots, core, near, far, moves, sem):
    def start(time, carry):
        slot = slots[time]
        chip = slot // 2
        mine = slot % 2 == core

        def copy(source):
            for number, (first, size, target) in enumerate(moves):
                rows = pl.ds(pl.multiple_of(time * size, size), size)
                pltpu.make_async_copy(source.at[chip, pl.ds(first, size)], target.at[rows], sem.at[number]).start()

        pl.when(mine)(lambda: copy(near))
        pl.when(jnp.logical_not(mine))(lambda: copy(far))
        return carry

    lax.fori_loop(0, FRAMES, start, 0)


def turn_values(staged, values, total):
    def turn(step, carry):
        rows = pl.ds(pl.multiple_of(step * WIDE, WIDE), WIDE)
        values[:, rows] = staged[rows].T
        return carry

    lax.fori_loop(0, total // WIDE, turn, 0)


def turn_queries(chips, staged, queries):
    for place in range(CHIPS):
        queries[place] = staged[chips[place]].T


def attend_kernel(info, near, far, bias, out, bits, *scratch):
    tops, totals, mixes, asked, queries, keys, staged, values, rim_keys, rim_staged, rim_values, slots, chips = scratch[:13]
    seen, items, rim_items, sem = scratch[13:17]
    raws = scratch[17:]
    raws, peaks = raws[: 2 * STREAMS], raws[2 * STREAMS :]
    raws, peaks = [(r[:STREAMS], r[STREAMS:]) for r in (raws, peaks)]
    core = info[FRAMES]
    for slot in range(FRAMES):
        slots[info[slot]] = slot
    ahead = jnp.int32(0)
    for chip in range(CHIPS):
        even = info[2 * chip]
        odd = info[2 * chip + 1]
        turned = (ahead >= 0) == (even > odd)
        bits[chip] = jnp.where(turned, 1, 0)
        ahead = ahead + jnp.where(turned, odd - even, even - odd)

        def ask(source):
            pltpu.make_async_copy(source.at[chip, pl.ds(0, TOKENS)], asked.at[chip], sem.at[4]).start()

        pl.when(turned)(lambda: ask(far))
        pl.when(jnp.logical_not(turned))(lambda: ask(near))
    rim_at = 3 * TOKENS
    moves = (
        (TOKENS, TOKENS, keys),
        (2 * TOKENS, TOKENS, staged),
        (rim_at, RIM, rim_keys),
        (rim_at + RIM, RIM, rim_staged),
    )
    gather_frames(slots, core, near, far, moves, sem)
    trip, rim_trip = plan(core, slots, bits, chips, seen, items, rim_items)
    tops[...] = jnp.full(tops.shape, LOWEST, jnp.float32)
    totals[...] = jnp.zeros(totals.shape, jnp.float32)
    mixes[...] = jnp.zeros(mixes.shape, jnp.float32)
    queries[pl.ds(CHIPS, STREAMS)] = jnp.zeros((STREAMS, HD, TOKENS), jnp.bfloat16)
    pltpu.make_async_copy(asked, asked, sem.at[4]).wait()
    turn_queries(chips, asked, queries)
    for number, move in enumerate(moves):
        pltpu.make_async_copy(move[2], move[2], sem.at[number]).wait()
    turn_values(staged, values, FRAMES * TOKENS)
    turn_values(rim_staged, rim_values, FRAMES * RIM)

    def scored(raw, rows, remain):
        return raw + jnp.where(remain <= 0, LOWEST, 0.0)

    sweep(trip, scored, queries, keys, values, tops, totals, mixes, items, seen, TOKENS, raws, peaks)

    def rim_scored(raw, rows, remain):
        place = lax.broadcasted_iota(jnp.int32, (PIECE, HD), 0)
        added = jnp.where(place < remain, bias[rows], LOWEST)
        return jnp.concatenate([raw[:, :HD] + added, raw[:, HD:] + added], axis=1)

    sweep(rim_trip, rim_scored, queries, rim_keys, rim_values, tops, totals, mixes, rim_items, seen, RIM, raws, peaks)
    for place in range(CHIPS):
        whole = jnp.sum(totals[place], axis=0, keepdims=True)
        out[chips[place]] = (mixes[place] / whole).T.astype(jnp.bfloat16)


def attend(info, near, far, bias):
    return pl.pallas_call(
        attend_kernel,
        grid_spec=pltpu.PrefetchScalarGridSpec(
            num_scalar_prefetch=1,
            grid=(1,),
            in_specs=[
                pl.BlockSpec(memory_space=pl.ANY),
                pl.BlockSpec(memory_space=pl.ANY),
                pl.BlockSpec(bias.shape, lambda i, info: (0, 0)),
            ],
            out_specs=[
                pl.BlockSpec((CHIPS, TOKENS, HD), lambda i, info: (0, 0, 0)),
                pl.BlockSpec(memory_space=pltpu.SMEM),
            ],
            scratch_shapes=[
                pltpu.VMEM((ROWS, 8, TOKENS), jnp.float32),
                pltpu.VMEM((ROWS, 8, TOKENS), jnp.float32),
                pltpu.VMEM((ROWS, HD, TOKENS), jnp.float32),
                pltpu.VMEM((CHIPS, TOKENS, HD), jnp.bfloat16),
                pltpu.VMEM((ROWS, HD, TOKENS), jnp.bfloat16),
                pltpu.VMEM((FRAMES * TOKENS, HD), jnp.bfloat16),
                pltpu.VMEM((FRAMES * TOKENS, HD), jnp.bfloat16),
                pltpu.VMEM((HD, FRAMES * TOKENS), jnp.bfloat16),
                pltpu.VMEM((FRAMES * RIM, HD), jnp.bfloat16),
                pltpu.VMEM((FRAMES * RIM, HD), jnp.bfloat16),
                pltpu.VMEM((HD, FRAMES * RIM), jnp.bfloat16),
                pltpu.SMEM((FRAMES,), jnp.int32),
                pltpu.SMEM((CHIPS + 2 * STREAMS,), jnp.int32),
                pltpu.SMEM((ROWS,), jnp.int32),
                pltpu.SMEM((STREAMS, LIMIT + 2), jnp.int32),
                pltpu.SMEM((STREAMS, LIMIT + 2), jnp.int32),
            ]
            + [pltpu.SemaphoreType.DMA((5,))]
            + [pltpu.VMEM((WIDE, TOKENS), jnp.float32)] * (2 * STREAMS)
            + [pltpu.VMEM((8, TOKENS), jnp.float32)] * (2 * STREAMS),
        ),
        out_shape=[
            jax.ShapeDtypeStruct((CHIPS, TOKENS, HD), jnp.bfloat16),
            jax.ShapeDtypeStruct((CHIPS,), jnp.int32),
        ],
        compiler_params=pltpu.CompilerParams(vmem_limit_bytes=48 * 1024 * 1024),
        name="attend",
    )(info, near, far, bias)


def swap_cores(value):
    return lax.ppermute(value, "ha", [(i, i ^ 1) for i in range(8)])


def swap_depth(value, bits):
    return lax.ppermute(value, "ha", [(i, i ^ (2 * bits)) for i in range(8)])


def rim_rows(sending, depth):
    lines = sending.reshape(2, SLOTS, LENGTH // TILE, TILE, HD)
    even = depth % 2 == 0
    upper = depth < 2

    def strip(tile, first):
        piece = lines[tile, :HEADS, TILE : 3 * TILE, first : first + PAD]
        return piece.reshape(HEADS, 2, TILE, PAD, HD)

    def bottom_or_top(value, axis):
        low = lax.slice_in_dim(value, TILE - PAD, TILE, axis=axis)
        return jnp.where(upper, low, lax.slice_in_dim(value, 0, PAD, axis=axis))

    def edge(first):
        low = lines[:, :HEADS, first + TILE - PAD : first + TILE]
        return jnp.where(upper, low, lines[:, :HEADS, first : first + PAD])

    sent = jnp.where(even, strip(1, TILE - PAD), strip(0, 0))
    outer = swap_depth(sent, 1)
    above = swap_depth(jnp.stack([edge(TILE), edge(2 * TILE)], axis=2), 2)
    corner = swap_depth(bottom_or_top(sent, 2), 3)
    inner = (strip(1, 0), strip(0, TILE - PAD))
    inner_corner = (above[1, :, :, :, :PAD], above[0, :, :, :, TILE - PAD :])
    spare = jnp.zeros((HEADS, 2, RIM - 104, HD), jnp.bfloat16)

    def flat(piece):
        return piece.reshape(HEADS, 2, -1, HD)

    both = []
    for tile in range(2):
        rows = [inner[tile], above[tile], inner_corner[tile], outer, corner]
        both.append(jnp.concatenate([flat(r) for r in rows] + [spare], axis=2))
    return jnp.stack(both).reshape(2, HEADS, 2 * RIM, HD)


def rim_bias(outer_valid):
    place = jnp.arange(RIM, dtype=jnp.int32)
    valid = (place < 68) | ((place < 104) & outer_valid)
    column_of = jnp.tile(jnp.where(valid, 0.0, LOWEST).astype(jnp.float32), FRAMES)
    return jnp.broadcast_to(column_of[:, None], (FRAMES * RIM, HD))


def finish_kernel(info, back, come, out):
    core = info[0]
    frame = jnp.where(core == info[1], 0, 1)
    for head in range(HEADS):
        columns = slice(head * HD, (head + 1) * HD)
        out[frame, :, columns] = back[core * SLOTS + head]
        out[1 - frame, :, columns] = come[head]


def finish(info, back, come):
    return pl.pallas_call(
        finish_kernel,
        grid_spec=pltpu.PrefetchScalarGridSpec(
            num_scalar_prefetch=1,
            grid=(1,),
            in_specs=[
                pl.BlockSpec((CHIPS, TOKENS, HD), lambda i, info: (0, 0, 0)),
                pl.BlockSpec((HEADS, TOKENS, HD), lambda i, info: (0, 0, 0)),
            ],
            out_specs=pl.BlockSpec((2, TOKENS, QD), lambda i, info: (0, 0, 0)),
        ),
        out_shape=jax.ShapeDtypeStruct((2, TOKENS, QD), jnp.bfloat16),
        compiler_params=pltpu.CompilerParams(vmem_limit_bytes=16 * 1024 * 1024),
        name="finish",
    )(info, back, come)


def shards(tokens, projection, norm_gain, modulation, levels, frame_order):
    chip = lax.axis_index("tm")
    place = lax.axis_index("ha")
    depth = place // 2
    core = place % 2
    sending, away = project(tokens.reshape(2, TOKENS, D), projection, norm_gain, modulation, levels, core)
    other = swap_cores(away)
    first = (1 - core) * SLOTS
    sending = lax.dynamic_update_slice(sending, other, (first, 0, 0))
    halves = sending.reshape(2, SLOTS, LENGTH, HD)
    halves = lax.dynamic_update_slice(halves, rim_rows(sending, depth), (0, 0, 3 * TOKENS, 0))
    sending = halves.reshape(CHIPS, LENGTH, HD)
    received = lax.all_to_all(sending, "tm", 0, 0, tiled=True)
    far = swap_cores(received)

    info = jnp.concatenate([frame_order, core[None]])
    odd_tile = chip // SLOTS
    bias = rim_bias(depth % 2 != odd_tile)
    mixed, bits = attend(info, received, far, bias)
    turned = lax.dynamic_index_in_dim(bits, chip, 0, keepdims=False)

    back = lax.all_to_all(mixed, "tm", 0, 0, tiled=True)
    leave = lax.dynamic_slice_in_dim(back, (1 - core) * SLOTS, HEADS, 0)
    come = swap_cores(leave)
    return finish(jnp.stack([core, turned]), back, come).reshape(2, 1, TILE, TILE, QD)


def solution(mesh):
    in_specs = (P("tm", "ha", None, None, None), P(), P(), P(), P("tm"), P())
    out_specs = P("tm", "ha", None, None, None)
    return jax.shard_map(shards, mesh=mesh, in_specs=in_specs, out_specs=out_specs, check_vma=False)
```

```python
import functools
import math

import jax
import jax.numpy as jnp
from jax import lax
from jax.experimental import pallas as pl
from jax.experimental.pallas import tpu as pltpu
from jax.sharding import PartitionSpec as P

D = 1536
HEADS = 6
HD = 128
TILE = 16
PAD = 2
TOKENS = TILE * TILE
QD = HEADS * HD
FRAMES = 32
CHIPS = 16
SLOTS = 8
RIM = 112
LENGTH = 3 * TOKENS + 2 * RIM
LOWEST = -1e30
LOG2E = math.log2(math.e)
SCALE = LOG2E / math.sqrt(HD)
AXES = ("tm", "ha")


def project_kernel(info, tokens_hbm, weights, gains, modulation, own, away, inputs, tokens, rows, sem):
    part = pl.program_id(0)
    core = info[0]

    def put(target, result):
        result = result.astype(jnp.bfloat16)
        for head in range(HEADS):
            target[head] = result[:, head * HD : (head + 1) * HD]

    def scaled(raw, row):
        return raw * lax.rsqrt(jnp.mean(raw * raw, axis=-1, keepdims=True) + 1e-06) * row

    def product(values):
        return jnp.dot(values, weights[...], preferred_element_type=jnp.float32)

    @pl.when(part == 0)
    def _():
        frames = (1 - core, core)
        copies = []
        for turn, frame in enumerate(frames):
            copies.append(pltpu.make_async_copy(modulation.at[info[1 + frame]], rows.at[turn], sem.at[2 + turn]))
            copies.append(pltpu.make_async_copy(tokens_hbm.at[frame], tokens.at[turn], sem.at[turn]))
        for copy in copies:
            copy.start()
        for copy in copies:
            copy.wait()
        for turn, target in enumerate((away, own)):
            values = tokens[turn].astype(jnp.float32)
            average = jnp.mean(values, axis=-1, keepdims=True)
            centred = values - average
            spread = jnp.mean(centred * centred, axis=-1, keepdims=True)
            normed = centred * lax.rsqrt(spread + 1e-06)
            modulated = (normed * (1.0 + rows[turn, 1:2, :]) + rows[turn, 0:1, :]).astype(jnp.bfloat16)
            inputs[turn * TOKENS : (turn + 1) * TOKENS] = modulated
            put(target, scaled(product(modulated), gains[0:1, :]))

    @pl.when(part == 1)
    def _():
        raw = scaled(product(inputs[...]), gains[1:2, :])
        put(away, raw[:TOKENS])
        put(own, raw[TOKENS:])

    @pl.when(part == 2)
    def _():
        raw = product(inputs[...])
        put(away, raw[:TOKENS])
        put(own, raw[TOKENS:])


def in_hbm(value):
    return pltpu.with_memory_space_constraint(value, pltpu.HBM)


def project(tokens, projection, norm_gain, modulation, levels, core):
    info = jnp.concatenate([core[None], levels])
    return pl.pallas_call(
        project_kernel,
        grid_spec=pltpu.PrefetchScalarGridSpec(
            num_scalar_prefetch=1,
            grid=(3,),
            in_specs=[
                pl.BlockSpec(memory_space=pltpu.HBM),
                pl.BlockSpec((D, QD), lambda p, info: (0, p)),
                pl.BlockSpec((2, QD), lambda p, info: (0, 0)),
                pl.BlockSpec(memory_space=pltpu.HBM),
            ],
            out_specs=[
                pl.BlockSpec((SLOTS, TOKENS, HD), lambda p, info: (info[0], p, 0)),
                pl.BlockSpec((HEADS, TOKENS, HD), lambda p, info: (0, p, 0)),
            ],
            scratch_shapes=[
                pltpu.VMEM((2 * TOKENS, D), jnp.bfloat16),
                pltpu.VMEM((2, TOKENS, D), jnp.bfloat16),
                pltpu.VMEM((2, 2, D), jnp.float32),
                pltpu.SemaphoreType.DMA((4,)),
            ],
        ),
        out_shape=[
            jax.ShapeDtypeStruct((CHIPS, LENGTH, HD), jnp.bfloat16),
            jax.ShapeDtypeStruct((HEADS, 3 * TOKENS, HD), jnp.bfloat16),
        ],
        compiler_params=pltpu.CompilerParams(vmem_limit_bytes=60 * 1024 * 1024),
        name="project",
    )(info, in_hbm(tokens), projection, in_hbm(norm_gain), in_hbm(modulation))


STREAMS = 4
EACH = CHIPS // STREAMS
WIDE = 512
PIECE = 256
LIMIT = EACH * (FRAMES * TOKENS // WIDE)
ROWS = STREAMS * (EACH + 1)


def plan(core, slots, bits, chips, seen, items, rim_items):
    sizes = ((TOKENS, items), (RIM, rim_items))

    def visit(turn, carry):
        place = carry[0]
        time = FRAMES - 1 - turn
        slot = slots[time]
        mine = (slot + bits[slot // 2] + core) % 2 == 0
        lane = place % (2 * STREAMS)
        stream = jnp.where(lane < STREAMS, lane, 2 * STREAMS - 1 - lane)
        row = place // STREAMS

        @pl.when(mine)
        def _():
            chips[row * STREAMS + stream] = slot // 2
            seen[row * STREAMS + stream] = time + 1
            for number, (size, target) in enumerate(sizes):
                count = ((time + 1) * size + WIDE - 1) // WIDE
                used = chips[CHIPS + number * STREAMS + stream]

                def fill(step, inner):
                    target[stream, used + step] = row * WIDE + step
                    return inner

                lax.fori_loop(0, count, fill, 0)
                chips[CHIPS + number * STREAMS + stream] = used + count

        return (place + jnp.where(mine, 1, 0),)

    for number in range(2 * STREAMS):
        chips[CHIPS + number] = 0
    for stream in range(STREAMS):
        seen[CHIPS + stream] = FRAMES
    lax.fori_loop(0, FRAMES, visit, (jnp.int32(0),))
    trips = []
    for number, (size, target) in enumerate(sizes):
        totals = [chips[CHIPS + number * STREAMS + stream] for stream in range(STREAMS)]
        trip = functools.reduce(jnp.maximum, totals)
        for stream in range(STREAMS):

            def clear(step, carry):
                target[stream, step] = EACH * WIDE
                return carry

            lax.fori_loop(totals[stream], trip + 2, clear, 0)
        trips.append(trip)
    return trips


def fold(values, combine):
    return combine(values.reshape(values.shape[0] // 8, 8, values.shape[1]), axis=0)


def sweep(trip, scored, queries, keys, values, tops, totals, mixes, items, seen, size, raws, peaks):
    def spots_of(step):
        spots = []
        for stream in range(STREAMS):
            item = items[stream, step]
            row = item // WIDE * STREAMS + stream
            first = pl.multiple_of(item % WIDE * WIDE, WIDE)
            spots.append((row, first, seen[row] * size - first))
        return spots

    def ask(spot, part):
        row, first, remain = spot
        rows = pl.ds(pl.multiple_of(first + part * PIECE, PIECE), PIECE)
        raw = jnp.dot(keys[rows], queries[row], preferred_element_type=jnp.float32)
        return scored(raw, rows, remain - part * PIECE)

    def advance(step, slot):
        now = spots_of(step)
        then = spots_of(step + 1)
        state = []
        for stream, (row, first, remain) in enumerate(now):
            highest = jnp.max(peaks[slot][stream][...], axis=0, keepdims=True) * SCALE
            top = tops[row]
            newest = jnp.maximum(top, highest)
            rescale = jnp.exp2(top - newest)
            state.append([newest, totals[row] * rescale, mixes[row] * rescale[0:1], None])
        for part in range(WIDE // PIECE):
            span = slice(part * PIECE, (part + 1) * PIECE)
            for stream, (row, first, remain) in enumerate(now):
                raw = ask(then[stream], part)
                raws[1 - slot][stream][span] = raw
                peak = fold(raw, jnp.max)
                held = state[stream]
                held[3] = peak if part == 0 else jnp.maximum(held[3], peak)
                weights = jnp.exp2(raws[slot][stream][span] * SCALE - held[0][0:1])
                held[1] = held[1] + fold(weights, jnp.sum)
                columns = pl.ds(pl.multiple_of(first + part * PIECE, PIECE), PIECE)
                held[2] = held[2] + jnp.dot(values[:, columns], weights.astype(jnp.bfloat16), preferred_element_type=jnp.float32)
        for stream, (row, first, remain) in enumerate(now):
            tops[row], totals[row], mixes[row], peaks[1 - slot][stream][...] = state[stream]

    def body(pair, carry):
        advance(2 * pair, 0)
        advance(2 * pair + 1, 1)
        return carry

    for stream, spot in enumerate(spots_of(0)):
        for part in range(WIDE // PIECE):
            raw = ask(spot, part)
            raws[0][stream][part * PIECE : (part + 1) * PIECE] = raw
            peak = fold(raw, jnp.max)
            peaks[0][stream][...] = peak if part == 0 else jnp.maximum(peaks[0][stream][...], peak)
    lax.fori_loop(0, (trip + 1) // 2, body, 0)


def gather_frames(slots, core, near, far, moves, sem):
    def start(time, carry):
        slot = slots[time]
        chip = slot // 2
        mine = slot % 2 == core

        def copy(source):
            for number, (first, size, target) in enumerate(moves):
                rows = pl.ds(pl.multiple_of(time * size, size), size)
                pltpu.make_async_copy(source.at[chip, pl.ds(first, size)], target.at[rows], sem.at[number]).start()

        pl.when(mine)(lambda: copy(near))
        pl.when(jnp.logical_not(mine))(lambda: copy(far))
        return carry

    lax.fori_loop(0, FRAMES, start, 0)


def turn_values(staged, values, total):
    def turn(step, carry):
        rows = pl.ds(pl.multiple_of(step * WIDE, WIDE), WIDE)
        values[:, rows] = staged[rows].T
        return carry

    lax.fori_loop(0, total // WIDE, turn, 0)


def turn_queries(chips, staged, queries):
    for place in range(CHIPS):
        queries[place] = staged[chips[place]].T


def attend_kernel(info, near, far, bias, out, bits, *scratch):
    tops, totals, mixes, asked, queries, keys, staged, values, rim_keys, rim_staged, rim_values, slots, chips = scratch[:13]
    seen, items, rim_items, sem = scratch[13:17]
    raws = scratch[17:]
    raws, peaks = raws[: 2 * STREAMS], raws[2 * STREAMS :]
    raws, peaks = [(r[:STREAMS], r[STREAMS:]) for r in (raws, peaks)]
    core = info[FRAMES]
    for slot in range(FRAMES):
        slots[info[slot]] = slot
    ahead = jnp.int32(0)
    for chip in range(CHIPS):
        even = info[2 * chip]
        odd = info[2 * chip + 1]
        turned = (ahead >= 0) == (even > odd)
        bits[chip] = jnp.where(turned, 1, 0)
        ahead = ahead + jnp.where(turned, odd - even, even - odd)

        def ask(source):
            pltpu.make_async_copy(source.at[chip, pl.ds(0, TOKENS)], asked.at[chip], sem.at[4]).start()

        pl.when(turned)(lambda: ask(far))
        pl.when(jnp.logical_not(turned))(lambda: ask(near))
    rim_at = 3 * TOKENS
    moves = (
        (TOKENS, TOKENS, keys),
        (2 * TOKENS, TOKENS, staged),
        (rim_at, RIM, rim_keys),
        (rim_at + RIM, RIM, rim_staged),
    )
    gather_frames(slots, core, near, far, moves, sem)
    trip, rim_trip = plan(core, slots, bits, chips, seen, items, rim_items)
    tops[...] = jnp.full(tops.shape, LOWEST, jnp.float32)
    totals[...] = jnp.zeros(totals.shape, jnp.float32)
    mixes[...] = jnp.zeros(mixes.shape, jnp.float32)
    queries[pl.ds(CHIPS, STREAMS)] = jnp.zeros((STREAMS, HD, TOKENS), jnp.bfloat16)
    pltpu.make_async_copy(asked, asked, sem.at[4]).wait()
    turn_queries(chips, asked, queries)
    for number, move in enumerate(moves):
        pltpu.make_async_copy(move[2], move[2], sem.at[number]).wait()
    turn_values(staged, values, FRAMES * TOKENS)
    turn_values(rim_staged, rim_values, FRAMES * RIM)

    def scored(raw, rows, remain):
        return raw + jnp.where(remain <= 0, LOWEST, 0.0)

    sweep(trip, scored, queries, keys, values, tops, totals, mixes, items, seen, TOKENS, raws, peaks)

    def rim_scored(raw, rows, remain):
        place = lax.broadcasted_iota(jnp.int32, (PIECE, HD), 0)
        added = jnp.where(place < remain, bias[rows], LOWEST)
        return jnp.concatenate([raw[:, :HD] + added, raw[:, HD:] + added], axis=1)

    sweep(rim_trip, rim_scored, queries, rim_keys, rim_values, tops, totals, mixes, rim_items, seen, RIM, raws, peaks)
    for place in range(CHIPS):
        whole = jnp.sum(totals[place], axis=0, keepdims=True)
        out[chips[place]] = (mixes[place] / whole).T.astype(jnp.bfloat16)


def attend(info, near, far, bias):
    return pl.pallas_call(
        attend_kernel,
        grid_spec=pltpu.PrefetchScalarGridSpec(
            num_scalar_prefetch=1,
            grid=(1,),
            in_specs=[
                pl.BlockSpec(memory_space=pl.ANY),
                pl.BlockSpec(memory_space=pl.ANY),
                pl.BlockSpec(bias.shape, lambda i, info: (0, 0)),
            ],
            out_specs=[
                pl.BlockSpec((CHIPS, TOKENS, HD), lambda i, info: (0, 0, 0)),
                pl.BlockSpec(memory_space=pltpu.SMEM),
            ],
            scratch_shapes=[
                pltpu.VMEM((ROWS, 8, TOKENS), jnp.float32),
                pltpu.VMEM((ROWS, 8, TOKENS), jnp.float32),
                pltpu.VMEM((ROWS, HD, TOKENS), jnp.float32),
                pltpu.VMEM((CHIPS, TOKENS, HD), jnp.bfloat16),
                pltpu.VMEM((ROWS, HD, TOKENS), jnp.bfloat16),
                pltpu.VMEM((FRAMES * TOKENS, HD), jnp.bfloat16),
                pltpu.VMEM((FRAMES * TOKENS, HD), jnp.bfloat16),
                pltpu.VMEM((HD, FRAMES * TOKENS), jnp.bfloat16),
                pltpu.VMEM((FRAMES * RIM, HD), jnp.bfloat16),
                pltpu.VMEM((FRAMES * RIM, HD), jnp.bfloat16),
                pltpu.VMEM((HD, FRAMES * RIM), jnp.bfloat16),
                pltpu.SMEM((FRAMES,), jnp.int32),
                pltpu.SMEM((CHIPS + 2 * STREAMS,), jnp.int32),
                pltpu.SMEM((ROWS,), jnp.int32),
                pltpu.SMEM((STREAMS, LIMIT + 2), jnp.int32),
                pltpu.SMEM((STREAMS, LIMIT + 2), jnp.int32),
            ]
            + [pltpu.SemaphoreType.DMA((5,))]
            + [pltpu.VMEM((WIDE, TOKENS), jnp.float32)] * (2 * STREAMS)
            + [pltpu.VMEM((8, TOKENS), jnp.float32)] * (2 * STREAMS),
        ),
        out_shape=[
            jax.ShapeDtypeStruct((CHIPS, TOKENS, HD), jnp.bfloat16),
            jax.ShapeDtypeStruct((CHIPS,), jnp.int32),
        ],
        compiler_params=pltpu.CompilerParams(vmem_limit_bytes=48 * 1024 * 1024),
        name="attend",
    )(info, near, far, bias)


def swap_cores(value):
    return lax.ppermute(value, "ha", [(i, i ^ 1) for i in range(8)])


def swap_depth(value, bits):
    return lax.ppermute(value, "ha", [(i, i ^ (2 * bits)) for i in range(8)])


def rim_rows(sending, depth):
    lines = sending.reshape(2, SLOTS, LENGTH // TILE, TILE, HD)
    even = depth % 2 == 0
    upper = depth < 2

    def strip(tile, first):
        piece = lines[tile, :HEADS, TILE : 3 * TILE, first : first + PAD]
        return piece.reshape(HEADS, 2, TILE, PAD, HD)

    def bottom_or_top(value, axis):
        low = lax.slice_in_dim(value, TILE - PAD, TILE, axis=axis)
        return jnp.where(upper, low, lax.slice_in_dim(value, 0, PAD, axis=axis))

    def edge(first):
        low = lines[:, :HEADS, first + TILE - PAD : first + TILE]
        return jnp.where(upper, low, lines[:, :HEADS, first : first + PAD])

    sent = jnp.where(even, strip(1, TILE - PAD), strip(0, 0))
    outer = swap_depth(sent, 1)
    above = swap_depth(jnp.stack([edge(TILE), edge(2 * TILE)], axis=2), 2)
    corner = swap_depth(bottom_or_top(sent, 2), 3)
    inner = (strip(1, 0), strip(0, TILE - PAD))
    inner_corner = (above[1, :, :, :, :PAD], above[0, :, :, :, TILE - PAD :])
    spare = jnp.zeros((HEADS, 2, RIM - 104, HD), jnp.bfloat16)

    def flat(piece):
        return piece.reshape(HEADS, 2, -1, HD)

    both = []
    for tile in range(2):
        rows = [inner[tile], above[tile], inner_corner[tile], outer, corner]
        both.append(jnp.concatenate([flat(r) for r in rows] + [spare], axis=2))
    return jnp.stack(both).reshape(2, HEADS, 2 * RIM, HD)


def rim_bias(outer_valid):
    place = jnp.arange(RIM, dtype=jnp.int32)
    valid = (place < 68) | ((place < 104) & outer_valid)
    column_of = jnp.tile(jnp.where(valid, 0.0, LOWEST).astype(jnp.float32), FRAMES)
    return jnp.broadcast_to(column_of[:, None], (FRAMES * RIM, HD))


def finish_kernel(info, back, come, out):
    core = lax.axis_index("ha") % 2
    frame = jnp.where(core == info[lax.axis_index("tm")], 0, 1)
    for head in range(HEADS):
        columns = slice(head * HD, (head + 1) * HD)
        out[frame, :, columns] = back[core * SLOTS + head]
        out[1 - frame, :, columns] = come[head]


def finish(info, back, come):
    return pl.pallas_call(
        finish_kernel,
        grid_spec=pltpu.PrefetchScalarGridSpec(
            num_scalar_prefetch=1,
            grid=(1,),
            in_specs=[
                pl.BlockSpec((CHIPS, TOKENS, HD), lambda i, info: (0, 0, 0)),
                pl.BlockSpec((HEADS, TOKENS, HD), lambda i, info: (0, 0, 0)),
            ],
            out_specs=pl.BlockSpec((2, TOKENS, QD), lambda i, info: (0, 0, 0)),
        ),
        out_shape=jax.ShapeDtypeStruct((2, TOKENS, QD), jnp.bfloat16),
        compiler_params=pltpu.CompilerParams(vmem_limit_bytes=16 * 1024 * 1024),
        name="finish",
    )(info, back, come)


def shards(tokens, projection, norm_gain, modulation, levels, frame_order):
    chip = lax.axis_index("tm")
    place = lax.axis_index("ha")
    depth = place // 2
    core = place % 2
    sending, away = project(tokens.reshape(2, TOKENS, D), projection, norm_gain, modulation, levels, core)
    other = swap_cores(away)
    first = (1 - core) * SLOTS
    sending = lax.dynamic_update_slice(sending, other, (first, 0, 0))
    halves = sending.reshape(2, SLOTS, LENGTH, HD)
    halves = lax.dynamic_update_slice(halves, rim_rows(sending, depth), (0, 0, 3 * TOKENS, 0))
    sending = halves.reshape(CHIPS, LENGTH, HD)
    received = lax.all_to_all(sending, "tm", 0, 0, tiled=True)
    far = swap_cores(received)

    info = jnp.concatenate([frame_order, core[None]])
    odd_tile = chip // SLOTS
    bias = rim_bias(depth % 2 != odd_tile)
    mixed, bits = attend(info, received, far, bias)

    back = lax.all_to_all(mixed, "tm", 0, 0, tiled=True)
    leave = lax.dynamic_slice_in_dim(back, (1 - core) * SLOTS, HEADS, 0)
    come = swap_cores(leave)
    return finish(bits, back, come).reshape(2, 1, TILE, TILE, QD)


def solution(mesh):
    in_specs = (P("tm", "ha", None, None, None), P(), P(), P(), P("tm"), P())
    out_specs = P("tm", "ha", None, None, None)
    return jax.shard_map(shards, mesh=mesh, in_specs=in_specs, out_specs=out_specs, check_vma=False)
```

```python
import functools
import math

import jax
import jax.numpy as jnp
from jax import lax
from jax.experimental import pallas as pl
from jax.experimental.pallas import tpu as pltpu
from jax.sharding import PartitionSpec as P

D = 1536
HEADS = 6
HD = 128
TILE = 16
PAD = 2
TOKENS = TILE * TILE
QD = HEADS * HD
FRAMES = 32
CHIPS = 16
SLOTS = 8
RIM = 112
LENGTH = 3 * TOKENS + 2 * RIM
LOWEST = -1e30
LOG2E = math.log2(math.e)
SCALE = LOG2E / math.sqrt(HD)
AXES = ("tm", "ha")


def project_kernel(info, tokens_hbm, weights, gains, modulation, own, away, inputs, tokens, rows, sem):
    part = pl.program_id(0)
    core = lax.axis_index("ha") % 2

    def put(target, result):
        result = result.astype(jnp.bfloat16)
        for head in range(HEADS):
            target[head] = result[:, head * HD : (head + 1) * HD]

    def scaled(raw, row):
        return raw * lax.rsqrt(jnp.mean(raw * raw, axis=-1, keepdims=True) + 1e-06) * row

    def product(values):
        return jnp.dot(values, weights[...], preferred_element_type=jnp.float32)

    @pl.when(part == 0)
    def _():
        frames = (1 - core, core)
        copies = []
        for turn, frame in enumerate(frames):
            copies.append(pltpu.make_async_copy(modulation.at[info[frame]], rows.at[turn], sem.at[2 + turn]))
            copies.append(pltpu.make_async_copy(tokens_hbm.at[frame], tokens.at[turn], sem.at[turn]))
        for copy in copies:
            copy.start()
        for copy in copies:
            copy.wait()
        for turn, target in enumerate((away, own)):
            values = tokens[turn].astype(jnp.float32)
            average = jnp.mean(values, axis=-1, keepdims=True)
            centred = values - average
            spread = jnp.mean(centred * centred, axis=-1, keepdims=True)
            normed = centred * lax.rsqrt(spread + 1e-06)
            modulated = (normed * (1.0 + rows[turn, 1:2, :]) + rows[turn, 0:1, :]).astype(jnp.bfloat16)
            inputs[turn * TOKENS : (turn + 1) * TOKENS] = modulated
            put(target, scaled(product(modulated), gains[0:1, :]))

    @pl.when(part == 1)
    def _():
        raw = scaled(product(inputs[...]), gains[1:2, :])
        put(away, raw[:TOKENS])
        put(own, raw[TOKENS:])

    @pl.when(part == 2)
    def _():
        raw = product(inputs[...])
        put(away, raw[:TOKENS])
        put(own, raw[TOKENS:])


def in_hbm(value):
    return pltpu.with_memory_space_constraint(value, pltpu.HBM)


def project(tokens, projection, norm_gain, modulation, levels, core):
    return pl.pallas_call(
        project_kernel,
        grid_spec=pltpu.PrefetchScalarGridSpec(
            num_scalar_prefetch=1,
            grid=(3,),
            in_specs=[
                pl.BlockSpec(memory_space=pltpu.HBM),
                pl.BlockSpec((D, QD), lambda p, info: (0, p)),
                pl.BlockSpec((2, QD), lambda p, info: (0, 0)),
                pl.BlockSpec(memory_space=pltpu.HBM),
            ],
            out_specs=[
                pl.BlockSpec((SLOTS, TOKENS, HD), lambda p, levels: (lax.axis_index("ha") % 2, p, 0)),
                pl.BlockSpec((HEADS, TOKENS, HD), lambda p, info: (0, p, 0)),
            ],
            scratch_shapes=[
                pltpu.VMEM((2 * TOKENS, D), jnp.bfloat16),
                pltpu.VMEM((2, TOKENS, D), jnp.bfloat16),
                pltpu.VMEM((2, 2, D), jnp.float32),
                pltpu.SemaphoreType.DMA((4,)),
            ],
        ),
        out_shape=[
            jax.ShapeDtypeStruct((CHIPS, LENGTH, HD), jnp.bfloat16),
            jax.ShapeDtypeStruct((HEADS, 3 * TOKENS, HD), jnp.bfloat16),
        ],
        compiler_params=pltpu.CompilerParams(vmem_limit_bytes=60 * 1024 * 1024),
        name="project",
    )(levels, in_hbm(tokens), projection, in_hbm(norm_gain), in_hbm(modulation))


STREAMS = 4
EACH = CHIPS // STREAMS
WIDE = 512
PIECE = 256
LIMIT = EACH * (FRAMES * TOKENS // WIDE)
ROWS = STREAMS * (EACH + 1)


def plan(core, slots, bits, chips, seen, items, rim_items):
    sizes = ((TOKENS, items), (RIM, rim_items))

    def visit(turn, carry):
        place = carry[0]
        time = FRAMES - 1 - turn
        slot = slots[time]
        mine = (slot + bits[slot // 2] + core) % 2 == 0
        lane = place % (2 * STREAMS)
        stream = jnp.where(lane < STREAMS, lane, 2 * STREAMS - 1 - lane)
        row = place // STREAMS

        @pl.when(mine)
        def _():
            chips[row * STREAMS + stream] = slot // 2
            seen[row * STREAMS + stream] = time + 1
            for number, (size, target) in enumerate(sizes):
                count = ((time + 1) * size + WIDE - 1) // WIDE
                used = chips[CHIPS + number * STREAMS + stream]

                def fill(step, inner):
                    target[stream, used + step] = row * WIDE + step
                    return inner

                lax.fori_loop(0, count, fill, 0)
                chips[CHIPS + number * STREAMS + stream] = used + count

        return (place + jnp.where(mine, 1, 0),)

    for number in range(2 * STREAMS):
        chips[CHIPS + number] = 0
    for stream in range(STREAMS):
        seen[CHIPS + stream] = FRAMES
    lax.fori_loop(0, FRAMES, visit, (jnp.int32(0),))
    trips = []
    for number, (size, target) in enumerate(sizes):
        totals = [chips[CHIPS + number * STREAMS + stream] for stream in range(STREAMS)]
        trip = functools.reduce(jnp.maximum, totals)
        for stream in range(STREAMS):

            def clear(step, carry):
                target[stream, step] = EACH * WIDE
                return carry

            lax.fori_loop(totals[stream], trip + 2, clear, 0)
        trips.append(trip)
    return trips


def fold(values, combine):
    return combine(values.reshape(values.shape[0] // 8, 8, values.shape[1]), axis=0)


def sweep(trip, scored, queries, keys, values, tops, totals, mixes, items, seen, size, raws, peaks):
    def spots_of(step):
        spots = []
        for stream in range(STREAMS):
            item = items[stream, step]
            row = item // WIDE * STREAMS + stream
            first = pl.multiple_of(item % WIDE * WIDE, WIDE)
            spots.append((row, first, seen[row] * size - first))
        return spots

    def ask(spot, part):
        row, first, remain = spot
        rows = pl.ds(pl.multiple_of(first + part * PIECE, PIECE), PIECE)
        raw = jnp.dot(keys[rows], queries[row], preferred_element_type=jnp.float32)
        return scored(raw, rows, remain - part * PIECE)

    def advance(step, slot):
        now = spots_of(step)
        then = spots_of(step + 1)
        state = []
        for stream, (row, first, remain) in enumerate(now):
            highest = jnp.max(peaks[slot][stream][...], axis=0, keepdims=True) * SCALE
            top = tops[row]
            newest = jnp.maximum(top, highest)
            rescale = jnp.exp2(top - newest)
            state.append([newest, totals[row] * rescale, mixes[row] * rescale[0:1], None])
        for part in range(WIDE // PIECE):
            span = slice(part * PIECE, (part + 1) * PIECE)
            for stream, (row, first, remain) in enumerate(now):
                raw = ask(then[stream], part)
                raws[1 - slot][stream][span] = raw
                peak = fold(raw, jnp.max)
                held = state[stream]
                held[3] = peak if part == 0 else jnp.maximum(held[3], peak)
                weights = jnp.exp2(raws[slot][stream][span] * SCALE - held[0][0:1])
                held[1] = held[1] + fold(weights, jnp.sum)
                columns = pl.ds(pl.multiple_of(first + part * PIECE, PIECE), PIECE)
                held[2] = held[2] + jnp.dot(values[:, columns], weights.astype(jnp.bfloat16), preferred_element_type=jnp.float32)
        for stream, (row, first, remain) in enumerate(now):
            tops[row], totals[row], mixes[row], peaks[1 - slot][stream][...] = state[stream]

    def body(pair, carry):
        advance(2 * pair, 0)
        advance(2 * pair + 1, 1)
        return carry

    for stream, spot in enumerate(spots_of(0)):
        for part in range(WIDE // PIECE):
            raw = ask(spot, part)
            raws[0][stream][part * PIECE : (part + 1) * PIECE] = raw
            peak = fold(raw, jnp.max)
            peaks[0][stream][...] = peak if part == 0 else jnp.maximum(peaks[0][stream][...], peak)
    lax.fori_loop(0, (trip + 1) // 2, body, 0)


def gather_frames(slots, core, near, far, moves, sem):
    def start(time, carry):
        slot = slots[time]
        chip = slot // 2
        mine = slot % 2 == core

        def copy(source):
            for number, (first, size, target) in enumerate(moves):
                rows = pl.ds(pl.multiple_of(time * size, size), size)
                pltpu.make_async_copy(source.at[chip, pl.ds(first, size)], target.at[rows], sem.at[number]).start()

        pl.when(mine)(lambda: copy(near))
        pl.when(jnp.logical_not(mine))(lambda: copy(far))
        return carry

    lax.fori_loop(0, FRAMES, start, 0)


def turn_values(staged, values, total):
    def turn(step, carry):
        rows = pl.ds(pl.multiple_of(step * WIDE, WIDE), WIDE)
        values[:, rows] = staged[rows].T
        return carry

    lax.fori_loop(0, total // WIDE, turn, 0)


def turn_queries(chips, staged, queries):
    for place in range(CHIPS):
        queries[place] = staged[chips[place]].T


def attend_kernel(info, near, far, bias, out, bits, *scratch):
    tops, totals, mixes, asked, queries, keys, staged, values, rim_keys, rim_staged, rim_values, slots, chips = scratch[:13]
    seen, items, rim_items, sem = scratch[13:17]
    raws = scratch[17:]
    raws, peaks = raws[: 2 * STREAMS], raws[2 * STREAMS :]
    raws, peaks = [(r[:STREAMS], r[STREAMS:]) for r in (raws, peaks)]
    core = lax.axis_index("ha") % 2
    for slot in range(FRAMES):
        slots[info[slot]] = slot
    ahead = jnp.int32(0)
    for chip in range(CHIPS):
        even = info[2 * chip]
        odd = info[2 * chip + 1]
        turned = (ahead >= 0) == (even > odd)
        bits[chip] = jnp.where(turned, 1, 0)
        ahead = ahead + jnp.where(turned, odd - even, even - odd)

        def ask(source):
            pltpu.make_async_copy(source.at[chip, pl.ds(0, TOKENS)], asked.at[chip], sem.at[4]).start()

        pl.when(turned)(lambda: ask(far))
        pl.when(jnp.logical_not(turned))(lambda: ask(near))
    rim_at = 3 * TOKENS
    moves = (
        (TOKENS, TOKENS, keys),
        (2 * TOKENS, TOKENS, staged),
        (rim_at, RIM, rim_keys),
        (rim_at + RIM, RIM, rim_staged),
    )
    gather_frames(slots, core, near, far, moves, sem)
    trip, rim_trip = plan(core, slots, bits, chips, seen, items, rim_items)
    tops[...] = jnp.full(tops.shape, LOWEST, jnp.float32)
    totals[...] = jnp.zeros(totals.shape, jnp.float32)
    mixes[...] = jnp.zeros(mixes.shape, jnp.float32)
    queries[pl.ds(CHIPS, STREAMS)] = jnp.zeros((STREAMS, HD, TOKENS), jnp.bfloat16)
    pltpu.make_async_copy(asked, asked, sem.at[4]).wait()
    turn_queries(chips, asked, queries)
    for number, move in enumerate(moves):
        pltpu.make_async_copy(move[2], move[2], sem.at[number]).wait()
    turn_values(staged, values, FRAMES * TOKENS)
    turn_values(rim_staged, rim_values, FRAMES * RIM)

    def scored(raw, rows, remain):
        return raw + jnp.where(remain <= 0, LOWEST, 0.0)

    sweep(trip, scored, queries, keys, values, tops, totals, mixes, items, seen, TOKENS, raws, peaks)

    def rim_scored(raw, rows, remain):
        place = lax.broadcasted_iota(jnp.int32, (PIECE, HD), 0)
        added = jnp.where(place < remain, bias[rows], LOWEST)
        return jnp.concatenate([raw[:, :HD] + added, raw[:, HD:] + added], axis=1)

    sweep(rim_trip, rim_scored, queries, rim_keys, rim_values, tops, totals, mixes, rim_items, seen, RIM, raws, peaks)
    for place in range(CHIPS):
        whole = jnp.sum(totals[place], axis=0, keepdims=True)
        out[chips[place]] = (mixes[place] / whole).T.astype(jnp.bfloat16)


def attend(info, near, far, bias):
    return pl.pallas_call(
        attend_kernel,
        grid_spec=pltpu.PrefetchScalarGridSpec(
            num_scalar_prefetch=1,
            grid=(1,),
            in_specs=[
                pl.BlockSpec(memory_space=pl.ANY),
                pl.BlockSpec(memory_space=pl.ANY),
                pl.BlockSpec(bias.shape, lambda i, info: (0, 0)),
            ],
            out_specs=[
                pl.BlockSpec((CHIPS, TOKENS, HD), lambda i, info: (0, 0, 0)),
                pl.BlockSpec(memory_space=pltpu.SMEM),
            ],
            scratch_shapes=[
                pltpu.VMEM((ROWS, 8, TOKENS), jnp.float32),
                pltpu.VMEM((ROWS, 8, TOKENS), jnp.float32),
                pltpu.VMEM((ROWS, HD, TOKENS), jnp.float32),
                pltpu.VMEM((CHIPS, TOKENS, HD), jnp.bfloat16),
                pltpu.VMEM((ROWS, HD, TOKENS), jnp.bfloat16),
                pltpu.VMEM((FRAMES * TOKENS, HD), jnp.bfloat16),
                pltpu.VMEM((FRAMES * TOKENS, HD), jnp.bfloat16),
                pltpu.VMEM((HD, FRAMES * TOKENS), jnp.bfloat16),
                pltpu.VMEM((FRAMES * RIM, HD), jnp.bfloat16),
                pltpu.VMEM((FRAMES * RIM, HD), jnp.bfloat16),
                pltpu.VMEM((HD, FRAMES * RIM), jnp.bfloat16),
                pltpu.SMEM((FRAMES,), jnp.int32),
                pltpu.SMEM((CHIPS + 2 * STREAMS,), jnp.int32),
                pltpu.SMEM((ROWS,), jnp.int32),
                pltpu.SMEM((STREAMS, LIMIT + 2), jnp.int32),
                pltpu.SMEM((STREAMS, LIMIT + 2), jnp.int32),
            ]
            + [pltpu.SemaphoreType.DMA((5,))]
            + [pltpu.VMEM((WIDE, TOKENS), jnp.float32)] * (2 * STREAMS)
            + [pltpu.VMEM((8, TOKENS), jnp.float32)] * (2 * STREAMS),
        ),
        out_shape=[
            jax.ShapeDtypeStruct((CHIPS, TOKENS, HD), jnp.bfloat16),
            jax.ShapeDtypeStruct((CHIPS,), jnp.int32),
        ],
        compiler_params=pltpu.CompilerParams(vmem_limit_bytes=48 * 1024 * 1024),
        name="attend",
    )(info, near, far, bias)


def swap_cores(value):
    return lax.ppermute(value, "ha", [(i, i ^ 1) for i in range(8)])


def swap_depth(value, bits):
    return lax.ppermute(value, "ha", [(i, i ^ (2 * bits)) for i in range(8)])


def rim_rows(sending, depth):
    lines = sending.reshape(2, SLOTS, LENGTH // TILE, TILE, HD)
    even = depth % 2 == 0
    upper = depth < 2

    def strip(tile, first):
        piece = lines[tile, :HEADS, TILE : 3 * TILE, first : first + PAD]
        return piece.reshape(HEADS, 2, TILE, PAD, HD)

    def bottom_or_top(value, axis):
        low = lax.slice_in_dim(value, TILE - PAD, TILE, axis=axis)
        return jnp.where(upper, low, lax.slice_in_dim(value, 0, PAD, axis=axis))

    def edge(first):
        low = lines[:, :HEADS, first + TILE - PAD : first + TILE]
        return jnp.where(upper, low, lines[:, :HEADS, first : first + PAD])

    sent = jnp.where(even, strip(1, TILE - PAD), strip(0, 0))
    outer = swap_depth(sent, 1)
    above = swap_depth(jnp.stack([edge(TILE), edge(2 * TILE)], axis=2), 2)
    corner = swap_depth(bottom_or_top(sent, 2), 3)
    inner = (strip(1, 0), strip(0, TILE - PAD))
    inner_corner = (above[1, :, :, :, :PAD], above[0, :, :, :, TILE - PAD :])
    spare = jnp.zeros((HEADS, 2, RIM - 104, HD), jnp.bfloat16)

    def flat(piece):
        return piece.reshape(HEADS, 2, -1, HD)

    both = []
    for tile in range(2):
        rows = [inner[tile], above[tile], inner_corner[tile], outer, corner]
        both.append(jnp.concatenate([flat(r) for r in rows] + [spare], axis=2))
    return jnp.stack(both).reshape(2, HEADS, 2 * RIM, HD)


def rim_bias(outer_valid):
    place = jnp.arange(RIM, dtype=jnp.int32)
    valid = (place < 68) | ((place < 104) & outer_valid)
    column_of = jnp.tile(jnp.where(valid, 0.0, LOWEST).astype(jnp.float32), FRAMES)
    return jnp.broadcast_to(column_of[:, None], (FRAMES * RIM, HD))


def finish_kernel(info, back, come, out):
    core = lax.axis_index("ha") % 2
    frame = jnp.where(core == info[lax.axis_index("tm")], 0, 1)
    for head in range(HEADS):
        columns = slice(head * HD, (head + 1) * HD)
        out[frame, :, columns] = back[core * SLOTS + head]
        out[1 - frame, :, columns] = come[head]


def finish(info, back, come):
    return pl.pallas_call(
        finish_kernel,
        grid_spec=pltpu.PrefetchScalarGridSpec(
            num_scalar_prefetch=1,
            grid=(1,),
            in_specs=[
                pl.BlockSpec((CHIPS, TOKENS, HD), lambda i, info: (0, 0, 0)),
                pl.BlockSpec((HEADS, TOKENS, HD), lambda i, info: (0, 0, 0)),
            ],
            out_specs=pl.BlockSpec((2, TOKENS, QD), lambda i, info: (0, 0, 0)),
        ),
        out_shape=jax.ShapeDtypeStruct((2, TOKENS, QD), jnp.bfloat16),
        compiler_params=pltpu.CompilerParams(vmem_limit_bytes=16 * 1024 * 1024),
        name="finish",
    )(info, back, come)


def shards(tokens, projection, norm_gain, modulation, levels, frame_order):
    chip = lax.axis_index("tm")
    place = lax.axis_index("ha")
    depth = place // 2
    core = place % 2
    sending, away = project(tokens.reshape(2, TOKENS, D), projection, norm_gain, modulation, levels, core)
    other = swap_cores(away)
    first = (1 - core) * SLOTS
    sending = lax.dynamic_update_slice(sending, other, (first, 0, 0))
    halves = sending.reshape(2, SLOTS, LENGTH, HD)
    halves = lax.dynamic_update_slice(halves, rim_rows(sending, depth), (0, 0, 3 * TOKENS, 0))
    sending = halves.reshape(CHIPS, LENGTH, HD)
    received = lax.all_to_all(sending, "tm", 0, 0, tiled=True)
    far = swap_cores(received)

    odd_tile = chip // SLOTS
    bias = rim_bias(depth % 2 != odd_tile)
    mixed, bits = attend(frame_order, received, far, bias)

    back = lax.all_to_all(mixed, "tm", 0, 0, tiled=True)
    leave = lax.dynamic_slice_in_dim(back, (1 - core) * SLOTS, HEADS, 0)
    come = swap_cores(leave)
    return finish(bits, back, come).reshape(2, 1, TILE, TILE, QD)


def solution(mesh):
    in_specs = (P("tm", "ha", None, None, None), P(), P(), P(), P("tm"), P())
    out_specs = P("tm", "ha", None, None, None)
    return jax.shard_map(shards, mesh=mesh, in_specs=in_specs, out_specs=out_specs, check_vma=False)
```
